32 devices in a mesh: region: 4 (over z), bulk: 8 (over y, x, core).
Axes of the slice: x: 2, y: 2, z: 4, core: 2. Of those that a mesh axis runs over, the one named last changes fastest.
Arguments:
- positions: float32 [2048, 3, 128], P(('region', 'bulk')), may hold values from -6 to 6
- fields: float32 [2048, 4, 128], P(('region', 'bulk')), may hold values from -6 to 6
- storage: float32 [2048, 128], P(('region', 'bulk')), may hold values from 0.5 to 2
- velocity: float32 [2048, 3, 128], P(('region', 'bulk')), may hold values from -4 to 4
- send_list: int32 [32, 3, 8, 1], P(('region', 'bulk')), may hold values from 0 to 63
- remote_local: int32 [32, 24, 2], P(('region', 'bulk')), may hold values from 0 to 63
- remote_mask: int32 [32, 24, 2, 16, 128], P(('region', 'bulk')), may hold values from 0 to 255
- local_pairs: int32 [32, 64, 2], P(('region', 'bulk')), may hold values from 0 to 63, as said below
- local_mask: int32 [32, 64, 16, 128], P(('region', 'bulk')), may hold values from 0 to 255
- migrate_list: int32 [32, 8, 1], P(('region', 'bulk')), may hold values from -1 to 63, as said below
Outputs:
- new_fields: float32 [2048, 4, 128], P(('region', 'bulk'))
- new_velocity: float32 [2048, 3, 128], P(('region', 'bulk'))
- arrived: float32 [256, 11, 128], P(('region', 'bulk'))
The draws below stay inside these ranges and needn't reach their ends.
Inputs may be any that keep to these rules, and one draw needn't show every extreme that they name: `local_pairs`: each pair names two different owned blocks. `migrate_list`: owned blocks named on one device are distinct; in each region some devices hand 1 blocks to each of several peers and the rest hand none.
All inputs are finite; a program needn't handle non-finite values.
Results may differ from the reference program's by a relative error of at most 0.00002.
Values sent between devices are 32-bit elements; how exact they have to be, the bound alone decides.
A program may use at most 64 MiB of HBM per device.

```python
import math
import jax
import jax.numpy as jnp
from jax import lax

PTS = 128
BLK_DEV = 64
SLOTS = 1
TOUCH = 2
MIG = 1
BLOCKS = 2048
RECV = 24
N_REGION = 4
N_BULK = 8


def mask_words(key, count):
    first_part = jax.random.randint(jax.random.fold_in(key, 1), (count, PTS // 8, PTS), 0, 256)
    second_part = jax.random.randint(jax.random.fold_in(key, 2), (count, PTS // 8, PTS), 0, 256)
    return jnp.bitwise_or(first_part, second_part).astype(jnp.int32)


def draw_remote_mask(key, part):
    key = jax.random.fold_in(key, 11)
    count = N_REGION * N_BULK * 3 * N_BULK * SLOTS * TOUCH
    return mask_words(key, count).reshape(N_REGION * N_BULK, 3 * N_BULK * SLOTS, TOUCH, PTS // 8, PTS)


def draw_local_mask(key, part):
    key = jax.random.fold_in(key, 17)
    count = N_REGION * N_BULK * BLK_DEV
    return mask_words(key, count).reshape(N_REGION * N_BULK, BLK_DEV, PTS // 8, PTS)


def draw_local_pairs(key, part):
    key = jax.random.fold_in(key, 23)
    first_block = jax.random.randint(jax.random.fold_in(key, 1), (N_REGION * N_BULK, BLK_DEV), 0, BLK_DEV)
    stride = jax.random.randint(jax.random.fold_in(key, 2), (N_REGION * N_BULK, BLK_DEV), 1, BLK_DEV)
    second_block = (first_block + stride) % BLK_DEV
    return jnp.stack([first_block, second_block], axis=-1).astype(jnp.int32)


def draw_migrate_list(key, part):
    key = jax.random.fold_in(key, 31)

    def one_device(device_key):
        return jax.random.permutation(device_key, BLK_DEV)[:N_BULK * MIG]

    def one_region(region_key):
        order = jax.random.permutation(jax.random.fold_in(region_key, 0), N_BULK)
        ranking = jnp.argsort(order)
        heavy = ranking < N_BULK // 2
        light = ranking >= N_BULK // 2
        device_keys = jax.random.split(jax.random.fold_in(region_key, 1), N_BULK)
        picks = jax.vmap(one_device)(device_keys).reshape(N_BULK, N_BULK, MIG)
        live = jnp.logical_and(heavy[:, None, None], light[None, :, None])
        return jnp.where(live, picks, -1)
    region_keys = jax.random.split(key, N_REGION)
    return jax.vmap(one_region)(region_keys).reshape(N_REGION * N_BULK, N_BULK, MIG).astype(jnp.int32)


def set_ends(result, own_key, smallest, largest):
    dims = result.shape
    place = [jax.random.randint(jax.random.fold_in(own_key, axis), (), 0, dims[axis]) for axis in range(len(dims))]
    result = result.at[tuple(place)].set(smallest)
    longest = dims.index(max(dims))
    place[longest] = (place[longest] + 1) % dims[longest]
    return result.at[tuple(place)].set(largest)


def steps_of(key, extent, cuts, low, top_value):
    level = 1.0
    for dim, shards_of in cuts:
        draws = jax.random.uniform(jax.random.fold_in(jax.random.fold_in(key, 6), dim), (shards_of,), jnp.float32, low / len(cuts), top_value / len(cuts))
        level = level * jnp.repeat(jnp.exp(draws), extent[dim] // shards_of).reshape((-1,) + (1,) * (len(extent) - 1 - dim))
    return level


def noise(rng, extent, scale, limit, cuts=(), kind=jnp.bfloat16):
    result = scale * jax.random.normal(rng, extent, jnp.float32)
    if cuts:
        result = result * steps_of(rng, extent, cuts, -0.22, 0.18)
    return jnp.clip(result, -limit, limit).astype(kind)


def setup_inputs(seed: int = 0) -> dict:
    key_list = jax.random.split(jax.random.key(seed), 11)
    return {
        "positions": noise(key_list[0], (BLOCKS, 3, PTS), 1.0, 6.0, ((0, 32),), jnp.float32),
        "fields": noise(key_list[1], (BLOCKS, 4, PTS), 1.0, 6.0, ((0, 32),), jnp.float32),
        "storage": jnp.clip(jnp.exp(math.log(2.0) - 1.3862944 * jax.random.uniform(key_list[2], (BLOCKS, PTS), jnp.float32) ** steps_of(key_list[2], (BLOCKS, PTS), ((0, 32),), -0.2, 0.2)), 0.5, 2.0),
        "velocity": noise(key_list[3], (BLOCKS, 3, PTS), 0.5, 4.0, ((0, 32),), jnp.float32),
        "send_list": set_ends(jax.random.randint(key_list[4], (N_REGION * N_BULK, 3, N_BULK, SLOTS), 0, BLK_DEV), jax.random.fold_in(key_list[4], 1), 0, BLK_DEV - 1).astype(jnp.int32),
        "remote_local": set_ends(jax.random.randint(key_list[5], (N_REGION * N_BULK, RECV, TOUCH), 0, BLK_DEV), jax.random.fold_in(key_list[5], 1), 0, BLK_DEV - 1).astype(jnp.int32),
        "remote_mask": draw_remote_mask(jax.random.fold_in(key_list[10], 71), 0),
        "local_pairs": draw_local_pairs(jax.random.fold_in(key_list[10], 71), 0),
        "local_mask": draw_local_mask(jax.random.fold_in(key_list[10], 71), 0),
        "migrate_list": draw_migrate_list(jax.random.fold_in(key_list[10], 71), 0),
    }


bond_stiff = 0.1
press_gain = 0.05
leak_gain = 0.5
time_step = 0.5
inv_horizon = 0.25
group_rows = 16


def unpack_bonds(packed):
    shifts = jnp.arange(8, dtype=jnp.int32)
    bit_table = jnp.bitwise_and(jnp.right_shift(packed[:, :, None, :], shifts[None, None, :, None]), 1)
    return bit_table.reshape(packed.shape[0], packed.shape[1] * 8, packed.shape[2]).astype(jnp.float32)


def tile_group(owned, others, packed):
    intact = unpack_bonds(packed)
    broken = 1.0 - intact
    apart = [others[:, k, :, None] - owned[:, k, None, :] for k in range(3)]
    dist_sq = apart[0] * apart[0] + apart[1] * apart[1] + apart[2] * apart[2]
    weight = 1.0 / (1.0 + inv_horizon * dist_sq)
    spring = bond_stiff * weight * intact
    leakage = weight * broken
    mean_press = 0.5 * (others[:, 6, :, None] + owned[:, 6, None, :])
    terms = [spring * (others[:, 3 + k, :, None] - owned[:, 3 + k, None, :]) - press_gain * leakage * mean_press * apart[k] for k in range(3)]
    terms.append(leak_gain * leakage * (others[:, 6, :, None] - owned[:, 6, None, :]))
    on_owned = jnp.stack([jnp.sum(t, axis=1) for t in terms], axis=1)
    on_others = jnp.stack([-jnp.sum(t, axis=2) for t in terms], axis=1)
    return on_owned, on_others


def tiles(owned, others, packed):
    count = owned.shape[0]
    groups = count // group_rows

    def one_group(items):
        return tile_group(items[0], items[1], items[2])

    on_owned, on_others = lax.map(one_group, (owned.reshape(groups, group_rows, 7, -1), others.reshape(groups, group_rows, 7, -1), packed.reshape(groups, group_rows, packed.shape[1], packed.shape[2])))
    return on_owned.reshape(count, 4, -1), on_others.reshape(count, 4, -1)


def device_terms(items):
    points, received, remote_local, remote_mask, local_pairs, local_mask = items
    slot_count, touch = remote_local.shape
    width = points.shape[2]
    flat_local = remote_local.reshape(-1)
    owned = points[flat_local]
    others = jnp.repeat(received, touch, axis=0)
    on_owned, on_others = tiles(owned, others, remote_mask.reshape(slot_count * touch, remote_mask.shape[2], remote_mask.shape[3]))
    totals = jnp.zeros((points.shape[0], 4, width), jnp.float32)
    totals = totals.at[flat_local].add(on_owned)
    slot_back = on_others.reshape(slot_count, touch, 4, width).sum(axis=1)
    first_block = local_pairs[:, 0]
    second_block = local_pairs[:, 1]
    pair_first, pair_second = tiles(points[first_block], points[second_block], local_mask)
    totals = totals.at[first_block].add(pair_first).at[second_block].add(pair_second)
    return totals, slot_back


def take_rows(source, picks):
    return source[picks]


def add_rows(totals, picks, terms):
    return totals.at[picks].add(terms)


def reference(positions, fields, storage, velocity, send_list, remote_local, remote_mask, local_pairs, local_mask, migrate_list):
    nreg = N_REGION
    nbulk = N_BULK
    points = jnp.concatenate([positions, fields], axis=1).reshape(nreg, nbulk, BLK_DEV, 7, PTS)
    sends = send_list.reshape(nreg, nbulk, 3, nbulk, SLOTS)
    pieces = []
    for direction in range(3):
        offset = direction - 1
        rolled_pts = jnp.roll(points, offset, axis=0)
        rolled_idx = jnp.roll(sends[:, :, direction], offset, axis=0).reshape(nreg, nbulk, nbulk * SLOTS)
        picked = jax.vmap(jax.vmap(take_rows))(rolled_pts, rolled_idx)
        picked = picked.reshape(nreg, nbulk, nbulk, SLOTS, 7, PTS).transpose(0, 2, 1, 3, 4, 5)
        pieces.append(picked)
    received = jnp.stack(pieces, axis=2).reshape(nreg * nbulk, 3 * nbulk * SLOTS, 7, PTS)
    totals, slot_back = lax.map(device_terms, (points.reshape(nreg * nbulk, BLK_DEV, 7, PTS), received, remote_local, remote_mask, local_pairs, local_mask))
    back = slot_back.reshape(nreg, nbulk, 3, nbulk, SLOTS, 4, PTS)
    totals = totals.reshape(nreg, nbulk, BLK_DEV, 4, PTS)
    for direction in range(3):
        offset = direction - 1
        piece = back[:, :, direction].transpose(0, 2, 1, 3, 4, 5)
        piece = jnp.roll(piece, -offset, axis=0).reshape(nreg, nbulk, nbulk * SLOTS, 4, PTS)
        picks = sends[:, :, direction].reshape(nreg, nbulk, nbulk * SLOTS)
        totals = jax.vmap(jax.vmap(add_rows))(totals, picks, piece)
    totals = totals.reshape(-1, 4, PTS)
    new_velocity = velocity + time_step * totals[:, :3]
    displace = fields[:, :3] + time_step * new_velocity
    pressure = fields[:, 3] + time_step * totals[:, 3] / storage
    new_fields = jnp.concatenate([displace, pressure[:, None, :]], axis=1)
    moving = jnp.concatenate([new_fields, new_velocity, positions, storage[:, None, :]], axis=1).reshape(nreg, nbulk, BLK_DEV, 11, PTS)
    moves = migrate_list.reshape(nreg, nbulk, nbulk * MIG)
    chosen = jax.vmap(jax.vmap(take_rows))(moving, jnp.maximum(moves, 0))
    chosen = jnp.where((moves >= 0)[..., None, None], chosen, 0.0)
    arrived = chosen.reshape(nreg, nbulk, nbulk, MIG, 11, PTS).transpose(0, 2, 1, 3, 4, 5).reshape(-1, 11, PTS)
    return new_fields, new_velocity, arrived
```

```python
import functools

import jax
import jax.numpy as jnp
from jax import lax
from jax.experimental import pallas as pl
from jax.experimental.pallas import tpu as pltpu
from jax.sharding import PartitionSpec as P

MESH = pl.DeviceIdType.MESH
bond_stiff = 0.1
leak_gain = 0.5
time_step = 0.5
half_press = 0.025
F32 = jnp.float32
BF16 = jnp.bfloat16


def rows_of(shape):
    return lax.broadcasted_iota(jnp.int32, shape, len(shape) - 2)


def roll(x, by):
    return pltpu.roll(x, by % 8, x.ndim - 2)


def top(x):
    return x.astype(BF16).astype(F32)


def split3(x):
    first = top(x)
    rest = x - first
    second = top(rest)
    return first, second, rest - second


def features(block):
    row = rows_of(block.shape)
    half = jnp.where(row < 3, 0.5 * block, 0.0)
    norm = jnp.sum(half * half, axis=-2, keepdims=True) + 0.5
    as_b = jnp.where(row == 3, norm, jnp.where(row == 4, 1.0, half))
    as_a = jnp.where(row == 3, 1.0, jnp.where(row == 4, norm, -2.0 * half))
    b1, b2, b3 = split3(as_b)
    a1, a2, a3 = split3(as_a)
    left = jnp.concatenate([b1, b1, b2, b2, b1, b3], axis=-2).astype(BF16)
    right = jnp.concatenate([a1, a2, a1, a2, a3, a1], axis=-2).astype(BF16)
    press = block[..., 6:7, :]
    moved = roll(block, -3)
    product = -0.25 * press * block
    product_top = top(product)
    moved_top = top(moved)
    block_top = top(block)
    press_top = top(press)
    spring_0 = jnp.where(row < 3, moved_top, jnp.where(row == 3, 1.0, 0.0))
    spring_1 = jnp.where((row >= 1) & (row < 4), roll(moved - moved_top, 1), 0.0)
    leak_0 = jnp.where(
        row < 3,
        product_top,
        jnp.where(
            row == 3, 0.0, jnp.where(row == 4, 1.0, jnp.where(row == 5, press_top, roll(block_top, 6)))
        ),
    )
    leak_1 = jnp.where(
        row == 0,
        roll(block_top, 6),
        jnp.where(
            row < 4,
            roll(product - product_top, 1),
            jnp.where(row == 4, press - press_top, roll(block - block_top, 5)),
        ),
    )
    sums = jnp.concatenate(
        [
            jnp.concatenate([spring_0, spring_1], axis=-2),
            jnp.concatenate([leak_0, leak_1], axis=-2),
        ],
        axis=-1,
    ).astype(BF16)
    return left, right, sums


def combine(block, out):
    row = rows_of(block.shape)
    r0, r1 = out[:8], out[8:]
    o1 = r0 + roll(r1, -1)
    o2 = r0[3:4]
    o4 = r0[4:5]
    o5 = r0[5:6] + r1[4:5]
    o3 = jnp.where(row < 2, roll(r0, 2), roll(r1, 2)) + roll(r1, 3)
    press = block[6:7]
    force = bond_stiff * (o1 - roll(block, -3) * o2) + half_press * (
        block * (press * o4 + o5) - press * o3
    )
    leak = leak_gain * (o5 - press * o4)
    return jnp.where(row < 3, force, jnp.where(row == 3, leak, 0.0))


def tile(left_b, right_a, sums_b, sums_a, packed):
    dist = lax.dot_general(
        left_b, right_a, (((0,), (0,)), ((), ())), preferred_element_type=F32
    )
    guess = pl.reciprocal(dist, approx=True)
    weight = guess * (2.0 - dist * guess)
    words, width = packed.shape
    bit = lax.shift_left(1, rows_of((1, 8, width)))
    intact = (jnp.broadcast_to(packed[:, None, :], (words, 8, width)) & bit) != 0
    intact = intact.reshape(words * 8, width)
    spring = jnp.where(intact, weight, 0.0)
    leak = jnp.where(intact, 0.0, weight)
    spring_hi = spring.astype(BF16)
    leak_hi = leak.astype(BF16)
    spring_lo = (spring - spring_hi.astype(F32)).astype(BF16)
    leak_lo = (leak - leak_hi.astype(F32)).astype(BF16)
    along_j = (((1,), (0,)), ((), ()))
    along_i = (((1,), (1,)), ((), ()))
    dot = functools.partial(lax.dot_general, preferred_element_type=F32)
    on_a = dot(sums_b, jnp.concatenate([spring_hi, leak_hi], axis=0), along_j) + dot(
        sums_b, jnp.concatenate([spring_lo, leak_lo], axis=0), along_j
    )
    on_b = dot(sums_a, jnp.concatenate([spring_hi, leak_hi], axis=1), along_i) + dot(
        sums_a, jnp.concatenate([spring_lo, leak_lo], axis=1), along_i
    )
    return on_a, on_b


def kernel(
    nreg,
    nbulk,
    pos_ref,
    fld_ref,
    sto_ref,
    vel_ref,
    send_s,
    touch_s,
    pair_s,
    move_s,
    send_v,
    touch_v,
    pair_v,
    rmask_ref,
    lmask_ref,
    nf_ref,
    nv_ref,
    arr_ref,
    pts,
    stage,
    got,
    back,
    ret,
    mstage,
    mgot,
    left,
    right,
    sums,
    terms,
    send1,
    recv1,
    send2,
    recv2,
    send3,
    recv3,
):
    blocks, width = sto_ref.shape
    slots = send_s.shape[1]
    per = nbulk * slots
    recv_count = 3 * per
    pairs = pair_s.shape[1]
    touch = touch_s.shape[0]
    mig = move_s.shape[0]
    r = lax.axis_index("region")
    me = lax.axis_index("bulk")

    def region_at(by):
        return lax.rem(r + by + nreg, nreg)

    peers = []
    for o in (0, 2, 1):
        for step in range(nbulk):
            if o == 1 and step == 0:
                continue
            peers.append((o, lax.rem(me + step, nbulk)))

    barrier = pltpu.get_barrier_semaphore()
    for o, d in peers:
        pl.semaphore_signal(barrier, inc=1, device_id=(region_at(o - 1), d), device_id_type=MESH)

    for k in range(3):
        pts[:, k, :] = pos_ref[k]
    for k in range(4):
        pts[:, 3 + k, :] = fld_ref[:, k, :]
    pts[:, 7, :] = jnp.zeros((blocks, width), F32)
    for o in range(3):
        for s in range(slots):
            for d in range(nbulk):
                stage[o, d * slots + s] = pts[send_s[o, s, d]]
    for s in range(slots):
        got[1, me * slots + s] = stage[1, me * slots + s]

    def span(ref, o, d):
        return ref.at[o, pl.ds(d * slots, slots)]

    def copy1(o, d):
        return pltpu.make_async_remote_copy(
            src_ref=span(stage, o, d),
            dst_ref=span(got, o, me),
            send_sem=send1.at[o, d],
            recv_sem=recv1.at[o, me],
            device_id=(region_at(o - 1), d),
            device_id_type=MESH,
        )

    def copy2(o, b):
        return pltpu.make_async_remote_copy(
            src_ref=span(back, o, b),
            dst_ref=span(ret, o, me),
            send_sem=send2.at[o, b],
            recv_sem=recv2.at[o, me],
            device_id=(region_at(1 - o), b),
            device_id_type=MESH,
        )

    def copy3(d):
        return pltpu.make_async_remote_copy(
            src_ref=mstage.at[pl.ds(d * mig, mig)],
            dst_ref=mgot.at[pl.ds(me * mig, mig)],
            send_sem=send3.at[d],
            recv_sem=recv3.at[me],
            device_id=(r, d),
            device_id_type=MESH,
        )

    def arrival(ref, sem, o, b):
        pltpu.make_async_copy(span(ref, o, b), span(ref, o, b), sem.at[o, b]).wait()

    pl.semaphore_wait(barrier, len(peers))
    for o, d in peers:
        copy1(o, d).start()

    group = 8

    def build(step, carry):
        at = pl.ds(step * group, group)
        left[at], right[at], sums[at] = features(pts[at])
        return carry

    lax.fori_loop(0, blocks // group, build, 0)
    base = 2 * pairs
    used = base + touch * recv_count + recv_count
    rows = terms.shape[1]
    terms[:, base:, :] = jnp.zeros((4, rows - base, width), F32)

    def put(t, value):
        terms[:, pl.ds(t, 1), :] = value[0:4].reshape(4, 1, width)

    def local(t):
        a = pair_s[0, t]
        b = pair_s[1, t]
        on_a, on_b = tile(left[b], right[a], sums[b], sums[a], lmask_ref[t])
        put(t, combine(pts[a], on_a))
        put(pairs + t, combine(pts[b], on_b))

    def locals_(step, carry):
        local(2 * step)
        local(2 * step + 1)
        return carry

    lax.fori_loop(0, pairs // 2, locals_, 0)

    def remote(q, carry):
        o = q // per
        b = lax.rem(q, per) // slots
        s = lax.rem(q, slots)
        own = (o == 1) & (b == me)

        if slots == 1:
            @pl.when(jnp.logical_not(own))
            def _():
                arrival(got, recv1, o, b)
        else:
            @pl.when(jnp.logical_not(own) & (s == 0))
            def _():
                arrival(got, recv1, o, b)

        block = got[o, lax.rem(q, per)]
        left_b, _, sums_b = features(block[None])
        total = None
        for t in range(touch):
            a = touch_s[t, q]
            on_a, on_b = tile(left_b[0], right[a], sums_b[0], sums[a], rmask_ref[q, t])
            put(base + t * recv_count + q, combine(pts[a], on_a))
            total = on_b if total is None else total + on_b
        back[o, lax.rem(q, per)] = combine(block, total)

        @pl.when(jnp.logical_not(own) & (s == slots - 1))
        def _():
            copy2(o, b).start()

        return carry

    lax.fori_loop(0, recv_count, remote, 0)
    for s in range(slots):
        ret[1, me * slots + s] = back[1, me * slots + s]
    for o, d in peers:
        arrival(ret, recv2, o, d)
    for o in range(3):
        for d in range(per):
            put(base + touch * recv_count + o * per + d, ret[o, d])

    index = jnp.concatenate(
        [pair_v[0:1], pair_v[1:2]]
        + [touch_v[t : t + 1] for t in range(touch)]
        + [send_v[o] for o in range(3)]
        + [jnp.full((1, rows - used), -1, jnp.int32)],
        axis=1,
    )
    here = lax.broadcasted_iota(jnp.int32, (blocks, rows), 0)
    pick = jnp.where(here == index, 1.0, 0.0).astype(BF16)
    totals = []
    for k in range(4):
        parts = split3(terms[k])
        totals.append(
            sum(jnp.dot(pick, part.astype(BF16), preferred_element_type=F32) for part in parts)
        )
    for k in range(3):
        speed = vel_ref[k] + time_step * totals[k]
        nv_ref[k] = speed
        nf_ref[:, k, :] = fld_ref[:, k, :] + time_step * speed
    nf_ref[:, 3, :] = fld_ref[:, 3, :] + time_step * totals[3] / sto_ref[...]

    for d in range(nbulk):
        for m in range(mig):
            entry = move_s[m, 0, d]
            at = jnp.maximum(entry, 0)
            live = entry >= 0
            slot = d * mig + m
            mstage[slot, 0:4] = jnp.where(live, nf_ref[at], 0.0)
            for k in range(3):
                mstage[slot, 4 + k : 5 + k] = jnp.where(live, nv_ref[k, pl.ds(at, 1), :], 0.0)
                mstage[slot, 7 + k : 8 + k] = jnp.where(live, pos_ref[k, pl.ds(at, 1), :], 0.0)
            mstage[slot, 10:11] = jnp.where(live, sto_ref[pl.ds(at, 1), :], 0.0)
            mstage[slot, 11:16] = jnp.zeros((5, width), F32)
    others = [lax.rem(me + step, nbulk) for step in range(1, nbulk)]
    for d in others:
        copy3(d).start()
    for m in range(mig):
        mgot[me * mig + m] = mstage[me * mig + m]
    for o, d in peers:
        copy1(o, d).wait_send()
        copy2(o, d).wait_send()
    for d in others:
        landed = mgot.at[pl.ds(d * mig, mig)]
        pltpu.make_async_copy(landed, landed, recv3.at[d]).wait()
    for k in range(11):
        arr_ref[k] = mgot[:, k, :]
    for d in others:
        copy3(d).wait_send()


def solution(mesh):
    nreg, nbulk = mesh.shape["region"], mesh.shape["bulk"]

    def per_device(
        positions,
        fields,
        storage,
        velocity,
        send_list,
        remote_local,
        remote_mask,
        local_pairs,
        local_mask,
        migrate_list,
    ):
        blocks, _, width = positions.shape
        slots = send_list.shape[3]
        recv_count, touch = remote_local.shape[1:]
        pairs = local_pairs.shape[1]
        mig = migrate_list.shape[2]
        per = nbulk * slots
        rows = -(-(2 * pairs + (touch + 1) * recv_count) // 128) * 128
        sends = send_list[0].transpose(0, 2, 1)
        touches = remote_local[0].T
        pair_rows = local_pairs[0].T
        moves = migrate_list[0].T[:, None, :]
        vmem = pl.BlockSpec(memory_space=pltpu.VMEM)
        smem = pl.BlockSpec(memory_space=pltpu.SMEM)
        dma = pltpu.SemaphoreType.DMA
        new_fields, speed, arrived = pl.pallas_call(
            functools.partial(kernel, nreg, nbulk),
            out_shape=(
                jax.ShapeDtypeStruct((blocks, 4, width), F32),
                jax.ShapeDtypeStruct((3, blocks, width), F32),
                jax.ShapeDtypeStruct((11, nbulk * mig, width), F32),
            ),
            in_specs=[vmem] * 4 + [smem] * 4 + [vmem] * 5,
            out_specs=(vmem, vmem, vmem),
            scratch_shapes=[
                pltpu.VMEM((blocks, 8, width), F32),
                pltpu.VMEM((3, per, 8, width), F32),
                pltpu.VMEM((3, per, 8, width), F32),
                pltpu.VMEM((3, per, 8, width), F32),
                pltpu.VMEM((3, per, 8, width), F32),
                pltpu.VMEM((nbulk * mig, 16, width), F32),
                pltpu.VMEM((nbulk * mig, 16, width), F32),
                pltpu.VMEM((blocks, 48, width), BF16),
                pltpu.VMEM((blocks, 48, width), BF16),
                pltpu.VMEM((blocks, 16, 2 * width), BF16),
                pltpu.VMEM((4, rows, width), F32),
                dma((3, nbulk)),
                dma((3, nbulk)),
                dma((3, nbulk)),
                dma((3, nbulk)),
                dma((nbulk,)),
                dma((nbulk,)),
            ],
            compiler_params=pltpu.CompilerParams(
                collective_id=0, has_side_effects=True, vmem_limit_bytes=32 << 20
            ),
        )(
            positions.transpose(1, 0, 2),
            fields,
            storage,
            velocity.transpose(1, 0, 2),
            sends,
            touches,
            pair_rows,
            moves,
            sends,
            touches,
            pair_rows,
            remote_mask[0],
            local_mask[0],
        )
        return new_fields, speed.transpose(1, 0, 2), arrived.transpose(1, 0, 2)

    both = ("region", "bulk")
    return jax.shard_map(
        per_device,
        mesh=mesh,
        in_specs=(
            P(both, None, None),
            P(both, None, None),
            P(both, None),
            P(both, None, None),
            P(both, None, None, None),
            P(both, None, None),
            P(both, None, None, None, None),
            P(both, None, None),
            P(both, None, None, None),
            P(both, None, None),
        ),
        out_specs=(
            P(both, None, None),
            P(both, None, None),
            P(both, None, None),
        ),
        check_vma=False,
    )
```

```python
import functools

import jax
import jax.numpy as jnp
from jax import lax
from jax.experimental import pallas as pl
from jax.experimental.pallas import tpu as pltpu
from jax.sharding import PartitionSpec as P

MESH = pl.DeviceIdType.MESH
bond_stiff = 0.1
leak_gain = 0.5
time_step = 0.5
half_press = 0.025
F32 = jnp.float32
BF16 = jnp.bfloat16


def rows_of(shape):
    return lax.broadcasted_iota(jnp.int32, shape, len(shape) - 2)


def roll(x, by):
    return pltpu.roll(x, by % 8, x.ndim - 2)


def top(x):
    return x.astype(BF16).astype(F32)


def split3(x):
    first = top(x)
    rest = x - first
    second = top(rest)
    return first, second, rest - second


def features(block):
    row = rows_of(block.shape)
    half = jnp.where(row < 3, 0.5 * block, 0.0)
    norm = jnp.sum(half * half, axis=-2, keepdims=True) + 0.5
    as_b = jnp.where(row == 3, norm, jnp.where(row == 4, 1.0, half))
    as_a = jnp.where(row == 3, 1.0, jnp.where(row == 4, norm, -2.0 * half))
    b1, b2, b3 = split3(as_b)
    a1, a2, a3 = split3(as_a)
    left = jnp.concatenate([b1, b1, b2, b2, b1, b3], axis=-2).astype(BF16)
    right = jnp.concatenate([a1, a2, a1, a2, a3, a1], axis=-2).astype(BF16)
    press = block[..., 6:7, :]
    moved = roll(block, -3)
    product = -0.25 * press * block
    product_top = top(product)
    moved_top = top(moved)
    block_top = top(block)
    press_top = top(press)
    spring_0 = jnp.where(row < 3, moved_top, jnp.where(row == 3, 1.0, 0.0))
    spring_1 = jnp.where((row >= 1) & (row < 4), roll(moved - moved_top, 1), 0.0)
    leak_0 = jnp.where(
        row < 3,
        product_top,
        jnp.where(
            row == 3, 0.0, jnp.where(row == 4, 1.0, jnp.where(row == 5, press_top, roll(block_top, 6)))
        ),
    )
    leak_1 = jnp.where(
        row == 0,
        roll(block_top, 6),
        jnp.where(
            row < 4,
            roll(product - product_top, 1),
            jnp.where(row == 4, press - press_top, roll(block - block_top, 5)),
        ),
    )
    sums = jnp.concatenate(
        [
            jnp.concatenate([spring_0, spring_1], axis=-2),
            jnp.concatenate([leak_0, leak_1], axis=-2),
        ],
        axis=-1,
    ).astype(BF16)
    return left, right, sums


def combine(block, out):
    row = rows_of(block.shape)
    r0, r1 = out[:8], out[8:]
    o1 = r0 + roll(r1, -1)
    o2 = r0[3:4]
    o4 = r0[4:5]
    o5 = r0[5:6] + r1[4:5]
    o3 = jnp.where(row < 2, roll(r0, 2), roll(r1, 2)) + roll(r1, 3)
    press = block[6:7]
    force = bond_stiff * (o1 - roll(block, -3) * o2) + half_press * (
        block * (press * o4 + o5) - press * o3
    )
    leak = leak_gain * (o5 - press * o4)
    return jnp.where(row < 3, force, jnp.where(row == 3, leak, 0.0))


ALONG_J = (((1,), (0,)), ((), ()))
ALONG_I = (((1,), (1,)), ((), ()))
dot = functools.partial(lax.dot_general, preferred_element_type=F32)


def distance(left_b, right_a):
    return dot(left_b, right_a, (((0,), (0,)), ((), ())))


def split_weights(dist, packed):
    guess = pl.reciprocal(dist, approx=True)
    weight = guess * (2.0 - dist * guess)
    words, width = packed.shape
    bit = lax.shift_left(1, rows_of((1, 8, width)))
    intact = (jnp.broadcast_to(packed[:, None, :], (words, 8, width)) & bit) != 0
    intact = intact.reshape(words * 8, width)
    spring = jnp.where(intact, weight, 0.0)
    leak = jnp.where(intact, 0.0, weight)
    spring_hi = spring.astype(BF16)
    leak_hi = leak.astype(BF16)
    spring_lo = (spring - spring_hi.astype(F32)).astype(BF16)
    leak_lo = (leak - leak_hi.astype(F32)).astype(BF16)
    return spring_hi, leak_hi, spring_lo, leak_lo


def kernel(
    nreg,
    nbulk,
    pos_hbm,
    fld_hbm,
    sto_hbm,
    vel_hbm,
    send_hbm,
    touch_hbm,
    pair_hbm,
    move_hbm,
    rmask_hbm,
    lmask_hbm,
    nf_ref,
    nv_ref,
    arr_ref,
    pos_ref,
    fld_ref,
    sto_ref,
    vel_ref,
    send_s,
    touch_s,
    pair_s,
    move_s,
    send_v,
    touch_v,
    pair_v,
    rmask_ref,
    lmask_ref,
    pts,
    stage,
    got,
    back,
    ret,
    mstage,
    mgot,
    left,
    right,
    sums,
    rleft,
    rsums,
    terms,
    dists,
    weights,
    load_sem,
    send1,
    recv1,
    send2,
    recv2,
    send3,
    recv3,
):
    blocks, width = sto_ref.shape
    slots = send_s.shape[1]
    per = nbulk * slots
    recv_count = 3 * per
    pairs = pair_s.shape[1]
    touch = touch_s.shape[0]
    mig = move_s.shape[0]
    r = lax.axis_index("region")
    me = lax.axis_index("bulk")

    def region_at(by):
        return lax.rem(r + by + nreg, nreg)

    peers = []
    for o in (0, 2, 1):
        for step in range(nbulk):
            if o == 1 and step == 0:
                continue
            peers.append((o, lax.rem(me + step, nbulk)))

    loads = {}
    for n, (name, src, dst) in enumerate(
        (
            ("send_s", send_hbm, send_s),
            ("pos", pos_hbm, pos_ref),
            ("fld", fld_hbm, fld_ref),
            ("pair_s", pair_hbm, pair_s),
            ("lmask", lmask_hbm, lmask_ref),
            ("touch_s", touch_hbm, touch_s),
            ("rmask", rmask_hbm, rmask_ref),
            ("vel", vel_hbm, vel_ref),
            ("sto", sto_hbm, sto_ref),
            ("move_s", move_hbm, move_s),
            ("send_v", send_hbm, send_v),
            ("touch_v", touch_hbm, touch_v),
            ("pair_v", pair_hbm, pair_v),
        )
    ):
        loads[name] = pltpu.make_async_copy(src, dst, load_sem.at[n])
        loads[name].start()

    barrier = pltpu.get_barrier_semaphore()
    for o, d in peers:
        pl.semaphore_signal(barrier, inc=1, device_id=(region_at(o - 1), d), device_id_type=MESH)

    loads["pos"].wait()
    loads["fld"].wait()
    for k in range(3):
        pts[:, k, :] = pos_ref[k]
    for k in range(4):
        pts[:, 3 + k, :] = fld_ref[:, k, :]
    pts[:, 7, :] = jnp.zeros((blocks, width), F32)
    loads["send_s"].wait()
    for o in range(3):
        for s in range(slots):
            for d in range(nbulk):
                stage[o, d * slots + s] = pts[send_s[o, s, d]]
    for s in range(slots):
        got[1, me * slots + s] = stage[1, me * slots + s]

    def span(ref, o, d):
        return ref.at[o, pl.ds(d * slots, slots)]

    def copy1(o, d):
        return pltpu.make_async_remote_copy(
            src_ref=span(stage, o, d),
            dst_ref=span(got, o, me),
            send_sem=send1.at[o, d],
            recv_sem=recv1.at[o, me],
            device_id=(region_at(o - 1), d),
            device_id_type=MESH,
        )

    def copy2(o, b):
        return pltpu.make_async_remote_copy(
            src_ref=span(back, o, b),
            dst_ref=span(ret, o, me),
            send_sem=send2.at[o, b],
            recv_sem=recv2.at[o, me],
            device_id=(region_at(1 - o), b),
            device_id_type=MESH,
        )

    def copy3(d):
        return pltpu.make_async_remote_copy(
            src_ref=mstage.at[pl.ds(d * mig, mig)],
            dst_ref=mgot.at[pl.ds(me * mig, mig)],
            send_sem=send3.at[d],
            recv_sem=recv3.at[me],
            device_id=(r, d),
            device_id_type=MESH,
        )

    def arrival(ref, sem, o, b):
        pltpu.make_async_copy(span(ref, o, b), span(ref, o, b), sem.at[o, b]).wait()

    pl.semaphore_wait(barrier, len(peers))
    for o, d in peers:
        copy1(o, d).start()

    group = 8

    def build(step, carry):
        at = pl.ds(step * group, group)
        left[at], right[at], sums[at] = features(pts[at])
        return carry

    lax.fori_loop(0, blocks // group, build, 0)
    base = 2 * pairs
    used = base + touch * recv_count + recv_count
    rows = terms.shape[1]
    terms[:, base:, :] = jnp.zeros((4, rows - base, width), F32)

    def put(t, value):
        terms[:, pl.ds(t, 1), :] = value[0:4].reshape(4, 1, width)

    def stages(first, count, measure, weigh, add):
        def body(i, carry):
            add(jnp.maximum(i - 2, first))
            weigh(jnp.clip(i - 1, first, first + count - 1))
            measure(jnp.minimum(i, first + count - 1))
            return carry

        lax.fori_loop(first, first + count + 2, body, 0)

    def weigh_into(u, packed):
        s_hi, l_hi, s_lo, l_lo = split_weights(dists[u], packed)
        weights[u, 0, 0:width] = s_hi
        weights[u, 0, width:] = l_hi
        weights[u, 1, 0:width] = s_lo
        weights[u, 1, width:] = l_lo

    def add_tile(u, sums_a, sums_b):
        on_a = dot(sums_b, weights[u, 0], ALONG_J) + dot(sums_b, weights[u, 1], ALONG_J)
        on_b = None
        for piece in range(2):
            both = jnp.concatenate([weights[u, piece, 0:width], weights[u, piece, width:]], axis=1)
            part = dot(sums_a, both, ALONG_I)
            on_b = part if on_b is None else on_b + part
        return on_a, on_b

    lane = 4

    def local_measure(i):
        for u in range(lane):
            t = lane * i + u
            dists[u] = distance(left[pair_s[1, t]], right[pair_s[0, t]])

    def local_weigh(i):
        for u in range(lane):
            weigh_into(u, lmask_ref[lane * i + u])

    def local_add(i):
        for u in range(lane):
            t = lane * i + u
            a = pair_s[0, t]
            b = pair_s[1, t]
            on_a, on_b = add_tile(u, sums[a], sums[b])
            put(t, combine(pts[a], on_a))
            put(pairs + t, combine(pts[b], on_b))

    loads["pair_s"].wait()
    loads["lmask"].wait()
    local_count = pairs // lane
    early = local_count // 2
    stages(0, early, local_measure, local_weigh, local_add)

    loads["touch_s"].wait()
    loads["rmask"].wait()
    for o, d in peers:
        arrival(got, recv1, o, d)
    for o in range(3):
        for step in range(per // group):
            at = pl.ds(step * group, group)
            to = pl.ds(o * per + step * group, group)
            rleft[to], _, rsums[to] = features(got[o, at])
    near = lane // touch

    def remote_measure(i):
        for v in range(near):
            q = near * i + v
            for t in range(touch):
                dists[touch * v + t] = distance(rleft[q], right[touch_s[t, q]])

    def remote_weigh(i):
        for v in range(near):
            for t in range(touch):
                weigh_into(touch * v + t, rmask_ref[near * i + v, t])

    def remote_add(i):
        for v in range(near):
            q = near * i + v
            total = None
            for t in range(touch):
                a = touch_s[t, q]
                on_a, on_b = add_tile(touch * v + t, sums[a], rsums[q])
                put(base + t * recv_count + q, combine(pts[a], on_a))
                total = on_b if total is None else total + on_b
            o = q // per
            at = lax.rem(q, per)
            back[o, at] = combine(got[o, at], total)

    stages(0, recv_count // near, remote_measure, remote_weigh, remote_add)
    for o, d in peers:
        copy2(o, d).start()
    for s in range(slots):
        ret[1, me * slots + s] = back[1, me * slots + s]
    stages(early, local_count - early, local_measure, local_weigh, local_add)

    loads["send_v"].wait()
    loads["touch_v"].wait()
    loads["pair_v"].wait()
    index = jnp.concatenate(
        [pair_v[0:1], pair_v[1:2]]
        + [touch_v[t : t + 1] for t in range(touch)]
        + [send_v[o, s : s + 1] for o in range(3) for s in range(slots)]
        + [jnp.full((1, rows - used), -1, jnp.int32)],
        axis=1,
    )
    here = lax.broadcasted_iota(jnp.int32, (blocks, rows), 0)
    pick = jnp.where(here == index, 1.0, 0.0).astype(BF16)
    for o, d in peers:
        arrival(ret, recv2, o, d)
    for o in range(3):
        for s in range(slots):
            for d in range(nbulk):
                put(base + touch * recv_count + (o * slots + s) * nbulk + d, ret[o, d * slots + s])
    totals = []
    for k in range(4):
        parts = split3(terms[k])
        totals.append(
            sum(jnp.dot(pick, part.astype(BF16), preferred_element_type=F32) for part in parts)
        )
    loads["vel"].wait()
    loads["sto"].wait()
    for k in range(3):
        speed = vel_ref[k] + time_step * totals[k]
        nv_ref[k] = speed
        nf_ref[:, k, :] = fld_ref[:, k, :] + time_step * speed
    nf_ref[:, 3, :] = fld_ref[:, 3, :] + time_step * totals[3] / sto_ref[...]

    loads["move_s"].wait()
    for d in range(nbulk):
        for m in range(mig):
            entry = move_s[m, 0, d]
            at = jnp.maximum(entry, 0)
            live = entry >= 0
            slot = d * mig + m
            mstage[slot, 0:4] = jnp.where(live, nf_ref[at], 0.0)
            for k in range(3):
                mstage[slot, 4 + k : 5 + k] = jnp.where(live, nv_ref[k, pl.ds(at, 1), :], 0.0)
                mstage[slot, 7 + k : 8 + k] = jnp.where(live, pos_ref[k, pl.ds(at, 1), :], 0.0)
            mstage[slot, 10:11] = jnp.where(live, sto_ref[pl.ds(at, 1), :], 0.0)
            mstage[slot, 11:16] = jnp.zeros((5, width), F32)
    others = [lax.rem(me + step, nbulk) for step in range(1, nbulk)]
    for d in others:
        copy3(d).start()
    for m in range(mig):
        mgot[me * mig + m] = mstage[me * mig + m]
    for o, d in peers:
        copy1(o, d).wait_send()
        copy2(o, d).wait_send()
    for d in others:
        landed = mgot.at[pl.ds(d * mig, mig)]
        pltpu.make_async_copy(landed, landed, recv3.at[d]).wait()
    for k in range(11):
        arr_ref[k] = mgot[:, k, :]
    for d in others:
        copy3(d).wait_send()


def solution(mesh):
    nreg, nbulk = mesh.shape["region"], mesh.shape["bulk"]

    def per_device(
        positions,
        fields,
        storage,
        velocity,
        send_list,
        remote_local,
        remote_mask,
        local_pairs,
        local_mask,
        migrate_list,
    ):
        blocks, _, width = positions.shape
        slots = send_list.shape[3]
        recv_count, touch = remote_local.shape[1:]
        pairs = local_pairs.shape[1]
        mig = migrate_list.shape[2]
        per = nbulk * slots
        rows = -(-(2 * pairs + (touch + 1) * recv_count) // 128) * 128
        sends = send_list[0].transpose(0, 2, 1)
        touches = remote_local[0].T
        pair_rows = local_pairs[0].T
        moves = migrate_list[0].T[:, None, :]
        vmem = pl.BlockSpec(memory_space=pltpu.VMEM)
        dma = pltpu.SemaphoreType.DMA
        new_fields, speed, arrived = pl.pallas_call(
            functools.partial(kernel, nreg, nbulk),
            out_shape=(
                jax.ShapeDtypeStruct((blocks, 4, width), F32),
                jax.ShapeDtypeStruct((3, blocks, width), F32),
                jax.ShapeDtypeStruct((11, nbulk * mig, width), F32),
            ),
            in_specs=[pl.BlockSpec(memory_space=pltpu.HBM)] * 10,
            out_specs=(vmem, vmem, vmem),
            scratch_shapes=[
                pltpu.VMEM((3, blocks, width), F32),
                pltpu.VMEM((blocks, 4, width), F32),
                pltpu.VMEM((blocks, width), F32),
                pltpu.VMEM((3, blocks, width), F32),
                pltpu.SMEM(sends.shape, jnp.int32),
                pltpu.SMEM(touches.shape, jnp.int32),
                pltpu.SMEM(pair_rows.shape, jnp.int32),
                pltpu.SMEM(moves.shape, jnp.int32),
                pltpu.VMEM(sends.shape, jnp.int32),
                pltpu.VMEM(touches.shape, jnp.int32),
                pltpu.VMEM(pair_rows.shape, jnp.int32),
                pltpu.VMEM(remote_mask.shape[1:], jnp.int32),
                pltpu.VMEM(local_mask.shape[1:], jnp.int32),
                pltpu.VMEM((blocks, 8, width), F32),
                pltpu.VMEM((3, per, 8, width), F32),
                pltpu.VMEM((3, per, 8, width), F32),
                pltpu.VMEM((3, per, 8, width), F32),
                pltpu.VMEM((3, per, 8, width), F32),
                pltpu.VMEM((nbulk * mig, 16, width), F32),
                pltpu.VMEM((nbulk * mig, 16, width), F32),
                pltpu.VMEM((blocks, 48, width), BF16),
                pltpu.VMEM((blocks, 48, width), BF16),
                pltpu.VMEM((blocks, 16, 2 * width), BF16),
                pltpu.VMEM((recv_count, 48, width), BF16),
                pltpu.VMEM((recv_count, 16, 2 * width), BF16),
                pltpu.VMEM((4, rows, width), F32),
                pltpu.VMEM((4, width, width), F32),
                pltpu.VMEM((4, 2, 2 * width, width), BF16),
                dma((13,)),
                dma((3, nbulk)),
                dma((3, nbulk)),
                dma((3, nbulk)),
                dma((3, nbulk)),
                dma((nbulk,)),
                dma((nbulk,)),
            ],
            compiler_params=pltpu.CompilerParams(
                collective_id=0, has_side_effects=True, vmem_limit_bytes=64 << 20
            ),
        )(
            positions.transpose(1, 0, 2),
            fields,
            storage,
            velocity.transpose(1, 0, 2),
            sends,
            touches,
            pair_rows,
            moves,
            remote_mask[0],
            local_mask[0],
        )
        return new_fields, speed.transpose(1, 0, 2), arrived.transpose(1, 0, 2)

    both = ("region", "bulk")
    return jax.shard_map(
        per_device,
        mesh=mesh,
        in_specs=(
            P(both, None, None),
            P(both, None, None),
            P(both, None),
            P(both, None, None),
            P(both, None, None, None),
            P(both, None, None),
            P(both, None, None, None, None),
            P(both, None, None),
            P(both, None, None, None),
            P(both, None, None),
        ),
        out_specs=(
            P(both, None, None),
            P(both, None, None),
            P(both, None, None),
        ),
        check_vma=False,
    )
```

```python
import functools

import jax
import jax.numpy as jnp
from jax import lax
from jax.experimental import pallas as pl
from jax.experimental.pallas import tpu as pltpu
from jax.sharding import PartitionSpec as P

MESH = pl.DeviceIdType.MESH
bond_stiff = 0.1
leak_gain = 0.5
time_step = 0.5
half_press = 0.025
LANES = 4
F32 = jnp.float32
BF16 = jnp.bfloat16


def rows_of(shape):
    return lax.broadcasted_iota(jnp.int32, shape, len(shape) - 2)


def roll(x, by):
    return pltpu.roll(x, by % 8, x.ndim - 2)


def top(x):
    return x.astype(BF16).astype(F32)


def split3(x):
    first = top(x)
    rest = x - first
    second = top(rest)
    return first, second, rest - second


def features(block):
    row = rows_of(block.shape)
    half = jnp.where(row < 3, 0.5 * block, 0.0)
    norm = jnp.sum(half * half, axis=-2, keepdims=True) + 0.5
    as_b = jnp.where(row == 3, norm, jnp.where(row == 4, 1.0, half))
    as_a = jnp.where(row == 3, 1.0, jnp.where(row == 4, norm, -2.0 * half))
    b1, b2, b3 = split3(as_b)
    a1, a2, a3 = split3(as_a)
    left = jnp.concatenate([b1, b1, b2, b2, b1, b3], axis=-2).astype(BF16)
    right = jnp.concatenate([a1, a2, a1, a2, a3, a1], axis=-2).astype(BF16)
    press = block[..., 6:7, :]
    moved = roll(block, -3)
    product = -0.25 * press * block
    product_top = top(product)
    moved_top = top(moved)
    block_top = top(block)
    press_top = top(press)
    spring_0 = jnp.where(row < 3, moved_top, jnp.where(row == 3, 1.0, 0.0))
    spring_1 = jnp.where((row >= 1) & (row < 4), roll(moved - moved_top, 1), 0.0)
    leak_0 = jnp.where(
        row < 3,
        product_top,
        jnp.where(
            row == 3, 0.0, jnp.where(row == 4, 1.0, jnp.where(row == 5, press_top, roll(block_top, 6)))
        ),
    )
    leak_1 = jnp.where(
        row == 0,
        roll(block_top, 6),
        jnp.where(
            row < 4,
            roll(product - product_top, 1),
            jnp.where(row == 4, press - press_top, roll(block - block_top, 5)),
        ),
    )
    sums = jnp.concatenate(
        [
            jnp.concatenate([spring_0, spring_1], axis=-2),
            jnp.concatenate([leak_0, leak_1], axis=-2),
        ],
        axis=-1,
    ).astype(BF16)
    return left, right, sums


def combine(block, out):
    row = rows_of(block.shape)
    r0, r1 = out[:8], out[8:]
    o1 = r0 + roll(r1, -1)
    o2 = r0[3:4]
    o4 = r0[4:5]
    o5 = r0[5:6] + r1[4:5]
    o3 = jnp.where(row < 2, roll(r0, 2), roll(r1, 2)) + roll(r1, 3)
    press = block[6:7]
    force = bond_stiff * (o1 - roll(block, -3) * o2) + half_press * (
        block * (press * o4 + o5) - press * o3
    )
    leak = leak_gain * (o5 - press * o4)
    return jnp.where(row < 3, force, jnp.where(row == 3, leak, 0.0))


ALONG_J = (((1,), (0,)), ((), ()))
ALONG_I = (((1,), (1,)), ((), ()))
dot = functools.partial(lax.dot_general, preferred_element_type=F32)


def distance(left_b, right_a):
    return dot(left_b, right_a, (((0,), (0,)), ((), ())))


def split_weights(dist, packed):
    guess = pl.reciprocal(dist, approx=True)
    weight = guess * (2.0 - dist * guess)
    words, width = packed.shape
    bit = lax.shift_left(1, rows_of((1, 8, width)))
    intact = (jnp.broadcast_to(packed[:, None, :], (words, 8, width)) & bit) != 0
    intact = intact.reshape(words * 8, width)
    spring = jnp.where(intact, weight, 0.0)
    leak = jnp.where(intact, 0.0, weight)
    spring_hi = spring.astype(BF16)
    leak_hi = leak.astype(BF16)
    spring_lo = (spring - spring_hi.astype(F32)).astype(BF16)
    leak_lo = (leak - leak_hi.astype(F32)).astype(BF16)
    return spring_hi, leak_hi, spring_lo, leak_lo


def kernel(
    nreg,
    nbulk,
    pos_hbm,
    fld_hbm,
    sto_hbm,
    vel_hbm,
    send_hbm,
    touch_hbm,
    pair_hbm,
    move_hbm,
    rmask_hbm,
    lmask_hbm,
    nf_ref,
    nv_ref,
    arr_ref,
    pos_ref,
    fld_ref,
    sto_ref,
    vel_ref,
    send_s,
    touch_s,
    pair_s,
    move_s,
    send_v,
    touch_v,
    pair_v,
    masks,
    pts,
    stage,
    got,
    back,
    ret,
    mstage,
    mgot,
    left,
    right,
    sums,
    tab,
    aterm,
    bterm,
    dists,
    weights,
    load_sem,
    send1,
    recv1,
    send2,
    recv2,
    send3,
    recv3,
):
    blocks, width = sto_ref.shape
    slots = send_s.shape[1]
    per = nbulk * slots
    recv_count = 3 * per
    pairs = pair_s.shape[1]
    touch = touch_s.shape[0]
    mig = move_s.shape[0]
    r = lax.axis_index("region")
    me = lax.axis_index("bulk")

    def region_at(by):
        return lax.rem(r + by + nreg, nreg)

    peers = []
    for o in (0, 2, 1):
        for step in range(nbulk):
            if o == 1 and step == 0:
                continue
            peers.append((o, lax.rem(me + step, nbulk)))

    loads = {}
    for n, (name, src, dst) in enumerate(
        (
            ("send_s", send_hbm, send_s),
            ("pos", pos_hbm, pos_ref),
            ("fld", fld_hbm, fld_ref),
            ("pair_s", pair_hbm, pair_s),
            ("lmask", lmask_hbm, masks.at[pl.ds(0, pairs)]),
            ("touch_s", touch_hbm, touch_s),
            ("rmask", rmask_hbm, masks.at[pl.ds(pairs, touch * recv_count)]),
            ("vel", vel_hbm, vel_ref),
            ("sto", sto_hbm, sto_ref),
            ("move_s", move_hbm, move_s),
            ("send_v", send_hbm, send_v),
            ("touch_v", touch_hbm, touch_v),
            ("pair_v", pair_hbm, pair_v),
        )
    ):
        loads[name] = pltpu.make_async_copy(src, dst, load_sem.at[n])
        loads[name].start()

    barrier = pltpu.get_barrier_semaphore()
    for o, d in peers:
        pl.semaphore_signal(barrier, inc=1, device_id=(region_at(o - 1), d), device_id_type=MESH)

    loads["pos"].wait()
    loads["fld"].wait()
    for k in range(3):
        pts[0:blocks, k, :] = pos_ref[k]
    for k in range(4):
        pts[0:blocks, 3 + k, :] = fld_ref[:, k, :]
    pts[0:blocks, 7, :] = jnp.zeros((blocks, width), F32)
    loads["send_s"].wait()
    for o in range(3):
        for s in range(slots):
            for d in range(nbulk):
                stage[o, d * slots + s] = pts[send_s[o, s, d]]
    for s in range(slots):
        got[1, me * slots + s] = stage[1, me * slots + s]

    def span(ref, o, d):
        return ref.at[o, pl.ds(d * slots, slots)]

    def copy1(o, d):
        return pltpu.make_async_remote_copy(
            src_ref=span(stage, o, d),
            dst_ref=span(got, o, me),
            send_sem=send1.at[o, d],
            recv_sem=recv1.at[o, me],
            device_id=(region_at(o - 1), d),
            device_id_type=MESH,
        )

    def copy2(o, b):
        return pltpu.make_async_remote_copy(
            src_ref=span(back, o, b),
            dst_ref=span(ret, o, me),
            send_sem=send2.at[o, b],
            recv_sem=recv2.at[o, me],
            device_id=(region_at(1 - o), b),
            device_id_type=MESH,
        )

    def copy3(d):
        return pltpu.make_async_remote_copy(
            src_ref=mstage.at[pl.ds(d * mig, mig)],
            dst_ref=mgot.at[pl.ds(me * mig, mig)],
            send_sem=send3.at[d],
            recv_sem=recv3.at[me],
            device_id=(r, d),
            device_id_type=MESH,
        )

    def arrival(ref, sem, o, b):
        pltpu.make_async_copy(span(ref, o, b), span(ref, o, b), sem.at[o, b]).wait()

    pl.semaphore_wait(barrier, len(peers))
    for o, d in peers:
        copy1(o, d).start()

    group = 8

    def build(step, carry):
        at = pl.ds(step * group, group)
        left[at], right[at], sums[at] = features(pts[at])
        return carry

    lax.fori_loop(0, blocks // group, build, 0)

    loads["pair_s"].wait()
    loads["touch_s"].wait()
    for t in range(pairs):
        tab[0, t] = pair_s[0, t]
        tab[1, t] = pair_s[1, t]
    for q in range(recv_count):
        for t in range(touch):
            tab[0, pairs + touch * q + t] = touch_s[t, q]
            tab[1, pairs + touch * q + t] = blocks + q
    loads["lmask"].wait()
    loads["rmask"].wait()

    local_groups = pairs // LANES
    remote_groups = touch * recv_count // LANES
    count = local_groups + remote_groups
    early = local_groups // 2
    begin = early
    done = early + remote_groups

    def first_tile(i):
        shifted = jnp.where(
            i < begin, i, jnp.where(i < done, i + (local_groups - early), i - remote_groups)
        )
        return LANES * shifted

    def measure(first):
        for u in range(0, LANES, 2):
            f, g = [], []
            for v in (u, u + 1):
                f.append(left[tab[1, first + v]])
                g.append(right[tab[0, first + v]])
            blank = jnp.zeros_like(g[0])
            lhs = jnp.concatenate(f, axis=0)
            rhs = jnp.concatenate(
                [
                    jnp.concatenate([g[0], blank], axis=1),
                    jnp.concatenate([blank, g[1]], axis=1),
                ],
                axis=0,
            )
            dists[u // 2] = distance(lhs, rhs)

    def weigh(first):
        for u in range(LANES):
            cols = slice((u % 2) * width, (u % 2 + 1) * width)
            s_hi, l_hi, s_lo, l_lo = split_weights(dists[u // 2, :, cols], masks[first + u])
            weights[u // 2, 0, 0:width, cols] = s_hi
            weights[u // 2, 0, width:, cols] = l_hi
            weights[u // 2, 1, 0:width, cols] = s_lo
            weights[u // 2, 1, width:, cols] = l_lo

    def add(first):
        for u in range(0, LANES, 2):
            ids = [[tab[side, first + v] for v in (u, u + 1)] for side in range(2)]
            v_a = jnp.concatenate([sums[at] for at in ids[0]], axis=0)
            v_b = jnp.concatenate([sums[at] for at in ids[1]], axis=0)
            on_a = on_b = None
            for piece in range(2):
                w = weights[u // 2, piece]
                turned = jnp.concatenate(
                    [
                        jnp.concatenate([w[:width, :width], w[width:, :width]], axis=1),
                        jnp.concatenate([w[:width, width:], w[width:, width:]], axis=1),
                    ],
                    axis=0,
                )
                part_a = dot(v_b, w, ALONG_J)
                part_b = dot(v_a, turned, ALONG_I)
                on_a = part_a if on_a is None else on_a + part_a
                on_b = part_b if on_b is None else on_b + part_b
            for v in range(2):
                rows16 = slice(16 * v, 16 * v + 16)
                cols = slice(v * width, (v + 1) * width)
                aterm[first + u + v] = combine(pts[ids[0][v]], on_a[rows16, cols])
                bterm[first + u + v] = combine(pts[ids[1][v]], on_b[rows16, cols])

    def body(i, carry):
        @pl.when(i == begin)
        def _():
            for o, d in peers:
                arrival(got, recv1, o, d)
            for o in range(3):
                for step in range(per // group):
                    block = got[o, step * group : (step + 1) * group]
                    to = pl.ds(blocks + o * per + step * group, group)
                    pts[to] = block
                    left[to], _, sums[to] = features(block)

        @pl.when(i == done + 2)
        def _():
            for o in range(3):
                for s in range(per):
                    at = pairs + touch * (o * per + s)
                    back[o, s] = sum(bterm[at + t] for t in range(touch))
            for o, d in peers:
                copy2(o, d).start()

        add(first_tile(jnp.maximum(i - 2, 0)))
        weigh(first_tile(jnp.clip(i - 1, 0, count - 1)))
        measure(first_tile(jnp.minimum(i, count - 1)))
        return carry

    lax.fori_loop(0, count + 2, body, 0)
    for s in range(slots):
        ret[1, me * slots + s] = back[1, me * slots + s]

    loads["send_v"].wait()
    loads["touch_v"].wait()
    loads["pair_v"].wait()
    used = 2 * pairs + (touch + 1) * recv_count
    rows = -(-used // 128) * 128
    index = jnp.concatenate(
        [pair_v[0:1], pair_v[1:2]]
        + [touch_v[t : t + 1] for t in range(touch)]
        + [send_v[o, s : s + 1] for o in range(3) for s in range(slots)]
        + [jnp.full((1, rows - used), -1, jnp.int32)],
        axis=1,
    )
    here = lax.broadcasted_iota(jnp.int32, (blocks, rows), 0)
    pick = jnp.where(here == index, 1.0, 0.0).astype(BF16)
    for o, d in peers:
        arrival(ret, recv2, o, d)

    def plane(k):
        found = [aterm[0:pairs, k, :], bterm[0:pairs, k, :]]
        found += [aterm[pl.ds(pairs + t, recv_count, touch), k, :] for t in range(touch)]
        if slots == 1:
            found += [ret[o, :, k, :] for o in range(3)]
        else:
            found += [
                ret[o, pl.ds(s, nbulk, slots), k, :] for o in range(3) for s in range(slots)
            ]
        return jnp.concatenate(found + [jnp.zeros((rows - used, width), F32)], axis=0)

    totals = []
    for k in range(4):
        parts = split3(plane(k))
        totals.append(
            sum(jnp.dot(pick, part.astype(BF16), preferred_element_type=F32) for part in parts)
        )
    loads["vel"].wait()
    loads["sto"].wait()
    for k in range(3):
        speed = vel_ref[k] + time_step * totals[k]
        nv_ref[k] = speed
        nf_ref[:, k, :] = fld_ref[:, k, :] + time_step * speed
    nf_ref[:, 3, :] = fld_ref[:, 3, :] + time_step * totals[3] / sto_ref[...]

    loads["move_s"].wait()
    for d in range(nbulk):
        for m in range(mig):
            entry = move_s[m, 0, d]
            at = jnp.maximum(entry, 0)
            live = entry >= 0
            slot = d * mig + m
            mstage[slot, 0:4] = jnp.where(live, nf_ref[at], 0.0)
            for k in range(3):
                mstage[slot, 4 + k : 5 + k] = jnp.where(live, nv_ref[k, pl.ds(at, 1), :], 0.0)
                mstage[slot, 7 + k : 8 + k] = jnp.where(live, pos_ref[k, pl.ds(at, 1), :], 0.0)
            mstage[slot, 10:11] = jnp.where(live, sto_ref[pl.ds(at, 1), :], 0.0)
            mstage[slot, 11:16] = jnp.zeros((5, width), F32)
    others = [lax.rem(me + step, nbulk) for step in range(1, nbulk)]
    for d in others:
        copy3(d).start()
    for m in range(mig):
        mgot[me * mig + m] = mstage[me * mig + m]
    for o, d in peers:
        copy1(o, d).wait_send()
        copy2(o, d).wait_send()
    for d in others:
        landed = mgot.at[pl.ds(d * mig, mig)]
        pltpu.make_async_copy(landed, landed, recv3.at[d]).wait()
    for k in range(11):
        arr_ref[k] = mgot[:, k, :]
    for d in others:
        copy3(d).wait_send()


def solution(mesh):
    nreg, nbulk = mesh.shape["region"], mesh.shape["bulk"]

    def per_device(
        positions,
        fields,
        storage,
        velocity,
        send_list,
        remote_local,
        remote_mask,
        local_pairs,
        local_mask,
        migrate_list,
    ):
        blocks, _, width = positions.shape
        slots = send_list.shape[3]
        recv_count, touch = remote_local.shape[1:]
        pairs = local_pairs.shape[1]
        mig = migrate_list.shape[2]
        per = nbulk * slots
        tiles = pairs + touch * recv_count
        held = blocks + recv_count
        sends = send_list[0].transpose(0, 2, 1)
        touches = remote_local[0].T
        pair_rows = local_pairs[0].T
        moves = migrate_list[0].T[:, None, :]
        vmem = pl.BlockSpec(memory_space=pltpu.VMEM)
        dma = pltpu.SemaphoreType.DMA
        new_fields, speed, arrived = pl.pallas_call(
            functools.partial(kernel, nreg, nbulk),
            out_shape=(
                jax.ShapeDtypeStruct((blocks, 4, width), F32),
                jax.ShapeDtypeStruct((3, blocks, width), F32),
                jax.ShapeDtypeStruct((11, nbulk * mig, width), F32),
            ),
            in_specs=[pl.BlockSpec(memory_space=pltpu.HBM)] * 10,
            out_specs=(vmem, vmem, vmem),
            scratch_shapes=[
                pltpu.VMEM((3, blocks, width), F32),
                pltpu.VMEM((blocks, 4, width), F32),
                pltpu.VMEM((blocks, width), F32),
                pltpu.VMEM((3, blocks, width), F32),
                pltpu.SMEM(sends.shape, jnp.int32),
                pltpu.SMEM(touches.shape, jnp.int32),
                pltpu.SMEM(pair_rows.shape, jnp.int32),
                pltpu.SMEM(moves.shape, jnp.int32),
                pltpu.VMEM(sends.shape, jnp.int32),
                pltpu.VMEM(touches.shape, jnp.int32),
                pltpu.VMEM(pair_rows.shape, jnp.int32),
                pltpu.VMEM((tiles,) + local_mask.shape[2:], jnp.int32),
                pltpu.VMEM((held, 8, width), F32),
                pltpu.VMEM((3, per, 8, width), F32),
                pltpu.VMEM((3, per, 8, width), F32),
                pltpu.VMEM((3, per, 8, width), F32),
                pltpu.VMEM((3, per, 8, width), F32),
                pltpu.VMEM((nbulk * mig, 16, width), F32),
                pltpu.VMEM((nbulk * mig, 16, width), F32),
                pltpu.VMEM((held, 48, width), BF16),
                pltpu.VMEM((blocks, 48, width), BF16),
                pltpu.VMEM((held, 16, 2 * width), BF16),
                pltpu.SMEM((2, tiles), jnp.int32),
                pltpu.VMEM((tiles, 8, width), F32),
                pltpu.VMEM((tiles, 8, width), F32),
                pltpu.VMEM((LANES // 2, width, 2 * width), F32),
                pltpu.VMEM((LANES // 2, 2, 2 * width, 2 * width), BF16),
                dma((13,)),
                dma((3, nbulk)),
                dma((3, nbulk)),
                dma((3, nbulk)),
                dma((3, nbulk)),
                dma((nbulk,)),
                dma((nbulk,)),
            ],
            compiler_params=pltpu.CompilerParams(
                collective_id=0, has_side_effects=True, vmem_limit_bytes=64 << 20
            ),
        )(
            positions.transpose(1, 0, 2),
            fields,
            storage,
            velocity.transpose(1, 0, 2),
            sends,
            touches,
            pair_rows,
            moves,
            remote_mask[0].reshape((touch * recv_count,) + remote_mask.shape[3:]),
            local_mask[0],
        )
        return new_fields, speed.transpose(1, 0, 2), arrived.transpose(1, 0, 2)

    both = ("region", "bulk")
    return jax.shard_map(
        per_device,
        mesh=mesh,
        in_specs=(
            P(both, None, None),
            P(both, None, None),
            P(both, None),
            P(both, None, None),
            P(both, None, None, None),
            P(both, None, None),
            P(both, None, None, None, None),
            P(both, None, None),
            P(both, None, None, None),
            P(both, None, None),
        ),
        out_specs=(
            P(both, None, None),
            P(both, None, None),
            P(both, None, None),
        ),
        check_vma=False,
    )
```

```python
import functools

import jax
import jax.numpy as jnp
from jax import lax
from jax.experimental import pallas as pl
from jax.experimental.pallas import tpu as pltpu
from jax.sharding import PartitionSpec as P

MESH = pl.DeviceIdType.MESH
bond_stiff = 0.1
leak_gain = 0.5
time_step = 0.5
half_press = 0.025
LANES = 8
F32 = jnp.float32
BF16 = jnp.bfloat16


def rows_of(shape):
    return lax.broadcasted_iota(jnp.int32, shape, len(shape) - 2)


def roll(x, by):
    return pltpu.roll(x, by % 8, x.ndim - 2)


def top(x):
    return x.astype(BF16).astype(F32)


def split3(x):
    first = top(x)
    rest = x - first
    second = top(rest)
    return first, second, rest - second


def features(block):
    row = rows_of(block.shape)
    half = jnp.where(row < 3, 0.5 * block, 0.0)
    norm = jnp.sum(half * half, axis=-2, keepdims=True) + 0.5
    as_b = jnp.where(row == 3, norm, jnp.where(row == 4, 1.0, half))
    as_a = jnp.where(row == 3, 1.0, jnp.where(row == 4, norm, -2.0 * half))
    b1, b2, b3 = split3(as_b)
    a1, a2, a3 = split3(as_a)
    left = jnp.concatenate([b1, b1, b2, b2, b1, b3], axis=-2).astype(BF16)
    right = jnp.concatenate([a1, a2, a1, a2, a3, a1], axis=-2).astype(BF16)
    press = block[..., 6:7, :]
    moved = roll(block, -3)
    product = -0.25 * press * block
    product_top = top(product)
    moved_top = top(moved)
    block_top = top(block)
    press_top = top(press)
    spring_0 = jnp.where(row < 3, moved_top, jnp.where(row == 3, 1.0, 0.0))
    spring_1 = jnp.where((row >= 1) & (row < 4), roll(moved - moved_top, 1), 0.0)
    leak_0 = jnp.where(
        row < 3,
        product_top,
        jnp.where(
            row == 3, 0.0, jnp.where(row == 4, 1.0, jnp.where(row == 5, press_top, roll(block_top, 6)))
        ),
    )
    leak_1 = jnp.where(
        row == 0,
        roll(block_top, 6),
        jnp.where(
            row < 4,
            roll(product - product_top, 1),
            jnp.where(row == 4, press - press_top, roll(block - block_top, 5)),
        ),
    )
    sums = jnp.concatenate(
        [
            jnp.concatenate([spring_0, spring_1], axis=-2),
            jnp.concatenate([leak_0, leak_1], axis=-2),
        ],
        axis=-1,
    ).astype(BF16)
    return left, right, sums


def combine(block, out):
    row = rows_of(block.shape)
    r0, r1 = out[:8], out[8:]
    o1 = r0 + roll(r1, -1)
    o2 = r0[3:4]
    o4 = r0[4:5]
    o5 = r0[5:6] + r1[4:5]
    o3 = jnp.where(row < 2, roll(r0, 2), roll(r1, 2)) + roll(r1, 3)
    press = block[6:7]
    force = bond_stiff * (o1 - roll(block, -3) * o2) + half_press * (
        block * (press * o4 + o5) - press * o3
    )
    leak = leak_gain * (o5 - press * o4)
    return jnp.where(row < 3, force, jnp.where(row == 3, leak, 0.0))


ALONG_J = (((1,), (0,)), ((), ()))
ALONG_I = (((1,), (1,)), ((), ()))
dot = functools.partial(lax.dot_general, preferred_element_type=F32)


def distance(left_b, right_a):
    return dot(left_b, right_a, (((0,), (0,)), ((), ())))


def split_weights(dist, packed):
    guess = pl.reciprocal(dist, approx=True)
    weight = guess * (2.0 - dist * guess)
    words, width = packed.shape
    bit = lax.shift_left(1, rows_of((1, 8, width)))
    intact = (jnp.broadcast_to(packed[:, None, :], (words, 8, width)) & bit) != 0
    intact = intact.reshape(words * 8, width)
    spring = jnp.where(intact, weight, 0.0)
    leak = jnp.where(intact, 0.0, weight)
    spring_hi = spring.astype(BF16)
    leak_hi = leak.astype(BF16)
    spring_lo = (spring - spring_hi.astype(F32)).astype(BF16)
    leak_lo = (leak - leak_hi.astype(F32)).astype(BF16)
    return spring_hi, leak_hi, spring_lo, leak_lo


def kernel(
    nreg,
    nbulk,
    pos_hbm,
    fld_hbm,
    sto_hbm,
    vel_hbm,
    send_hbm,
    touch_hbm,
    pair_hbm,
    move_hbm,
    rmask_hbm,
    lmask_hbm,
    nf_ref,
    nv_ref,
    arr_ref,
    pos_ref,
    fld_ref,
    sto_ref,
    vel_ref,
    send_s,
    touch_s,
    pair_s,
    move_s,
    send_v,
    touch_v,
    pair_v,
    masks,
    pts,
    stage,
    got,
    back,
    ret,
    mstage,
    mgot,
    left,
    right,
    sums,
    tab,
    aterm,
    bterm,
    dists,
    weights,
    load_sem,
    send1,
    recv1,
    send2,
    recv2,
    send3,
    recv3,
):
    blocks, width = sto_ref.shape
    slots = send_s.shape[1]
    per = nbulk * slots
    recv_count = 3 * per
    pairs = pair_s.shape[1]
    touch = touch_s.shape[0]
    mig = move_s.shape[0]
    r = lax.axis_index("region")
    me = lax.axis_index("bulk")

    def region_at(by):
        return lax.rem(r + by + nreg, nreg)

    peers = []
    for o in (0, 2, 1):
        for step in range(nbulk):
            if o == 1 and step == 0:
                continue
            peers.append((o, lax.rem(me + step, nbulk)))

    loads = {}
    for n, (name, src, dst) in enumerate(
        (
            ("send_s", send_hbm, send_s),
            ("pos", pos_hbm, pos_ref),
            ("fld", fld_hbm, fld_ref),
            ("pair_s", pair_hbm, pair_s),
            ("lmask", lmask_hbm, masks.at[pl.ds(0, pairs)]),
            ("touch_s", touch_hbm, touch_s),
            ("rmask", rmask_hbm, masks.at[pl.ds(pairs, touch * recv_count)]),
            ("vel", vel_hbm, vel_ref),
            ("sto", sto_hbm, sto_ref),
            ("move_s", move_hbm, move_s),
            ("send_v", send_hbm, send_v),
            ("touch_v", touch_hbm, touch_v),
            ("pair_v", pair_hbm, pair_v),
        )
    ):
        loads[name] = pltpu.make_async_copy(src, dst, load_sem.at[n])
        loads[name].start()

    barrier = pltpu.get_barrier_semaphore()
    for o, d in peers:
        pl.semaphore_signal(barrier, inc=1, device_id=(region_at(o - 1), d), device_id_type=MESH)

    loads["pos"].wait()
    loads["fld"].wait()
    for k in range(3):
        pts[0:blocks, k, :] = pos_ref[k]
    for k in range(4):
        pts[0:blocks, 3 + k, :] = fld_ref[:, k, :]
    pts[0:blocks, 7, :] = jnp.zeros((blocks, width), F32)
    loads["send_s"].wait()
    for o in range(3):
        for s in range(slots):
            for d in range(nbulk):
                stage[o, d * slots + s] = pts[send_s[o, s, d]]
    for s in range(slots):
        got[1, me * slots + s] = stage[1, me * slots + s]

    def span(ref, o, d):
        return ref.at[o, pl.ds(d * slots, slots)]

    def copy1(o, d):
        return pltpu.make_async_remote_copy(
            src_ref=span(stage, o, d),
            dst_ref=span(got, o, me),
            send_sem=send1.at[o, d],
            recv_sem=recv1.at[o, me],
            device_id=(region_at(o - 1), d),
            device_id_type=MESH,
        )

    def copy2(o, b):
        return pltpu.make_async_remote_copy(
            src_ref=span(back, o, b),
            dst_ref=span(ret, o, me),
            send_sem=send2.at[o, b],
            recv_sem=recv2.at[o, me],
            device_id=(region_at(1 - o), b),
            device_id_type=MESH,
        )

    def copy3(d):
        return pltpu.make_async_remote_copy(
            src_ref=mstage.at[pl.ds(d * mig, mig)],
            dst_ref=mgot.at[pl.ds(me * mig, mig)],
            send_sem=send3.at[d],
            recv_sem=recv3.at[me],
            device_id=(r, d),
            device_id_type=MESH,
        )

    def arrival(ref, sem, o, b):
        pltpu.make_async_copy(span(ref, o, b), span(ref, o, b), sem.at[o, b]).wait()

    pl.semaphore_wait(barrier, len(peers))
    for o, d in peers:
        copy1(o, d).start()

    group = 8

    def build(step, carry):
        at = pl.ds(step * group, group)
        left[at], right[at], sums[at] = features(pts[at])
        return carry

    lax.fori_loop(0, blocks // group, build, 0)

    loads["pair_s"].wait()
    loads["touch_s"].wait()
    for t in range(pairs):
        tab[0, t] = pair_s[0, t]
        tab[1, t] = pair_s[1, t]
    for q in range(recv_count):
        for t in range(touch):
            tab[0, pairs + touch * q + t] = touch_s[t, q]
            tab[1, pairs + touch * q + t] = blocks + q
    loads["lmask"].wait()
    loads["rmask"].wait()

    local_groups = pairs // LANES
    remote_groups = touch * recv_count // LANES
    count = local_groups + remote_groups
    early = local_groups // 2
    begin = early
    done = early + remote_groups

    def first_tile(i):
        shifted = jnp.where(
            i < begin, i, jnp.where(i < done, i + (local_groups - early), i - remote_groups)
        )
        return LANES * shifted

    def measure(first):
        for u in range(0, LANES, 2):
            f, g = [], []
            for v in (u, u + 1):
                f.append(left[tab[1, first + v]])
                g.append(right[tab[0, first + v]])
            blank = jnp.zeros_like(g[0])
            lhs = jnp.concatenate(f, axis=0)
            rhs = jnp.concatenate(
                [
                    jnp.concatenate([g[0], blank], axis=1),
                    jnp.concatenate([blank, g[1]], axis=1),
                ],
                axis=0,
            )
            dists[u // 2] = distance(lhs, rhs)

    def weigh(first):
        for u in range(LANES):
            cols = slice((u % 2) * width, (u % 2 + 1) * width)
            s_hi, l_hi, s_lo, l_lo = split_weights(dists[u // 2, :, cols], masks[first + u])
            weights[u // 2, 0, 0:width, cols] = s_hi
            weights[u // 2, 0, width:, cols] = l_hi
            weights[u // 2, 1, 0:width, cols] = s_lo
            weights[u // 2, 1, width:, cols] = l_lo

    def add(first):
        for u in range(0, LANES, 2):
            ids = [[tab[side, first + v] for v in (u, u + 1)] for side in range(2)]
            v_a = jnp.concatenate([sums[at] for at in ids[0]], axis=0)
            v_b = jnp.concatenate([sums[at] for at in ids[1]], axis=0)
            on_a = on_b = None
            for piece in range(2):
                w = weights[u // 2, piece]
                turned = jnp.concatenate(
                    [
                        jnp.concatenate([w[:width, :width], w[width:, :width]], axis=1),
                        jnp.concatenate([w[:width, width:], w[width:, width:]], axis=1),
                    ],
                    axis=0,
                )
                part_a = dot(v_b, w, ALONG_J)
                part_b = dot(v_a, turned, ALONG_I)
                on_a = part_a if on_a is None else on_a + part_a
                on_b = part_b if on_b is None else on_b + part_b
            for v in range(2):
                rows16 = slice(16 * v, 16 * v + 16)
                cols = slice(v * width, (v + 1) * width)
                aterm[first + u + v] = combine(pts[ids[0][v]], on_a[rows16, cols])
                bterm[first + u + v] = combine(pts[ids[1][v]], on_b[rows16, cols])

    def body(i, carry):
        @pl.when(i == begin)
        def _():
            for o, d in peers:
                arrival(got, recv1, o, d)
            for o in range(3):
                for step in range(per // group):
                    block = got[o, step * group : (step + 1) * group]
                    to = pl.ds(blocks + o * per + step * group, group)
                    pts[to] = block
                    left[to], _, sums[to] = features(block)

        @pl.when(i == done + 2)
        def _():
            for o in range(3):
                for s in range(per):
                    at = pairs + touch * (o * per + s)
                    back[o, s] = sum(bterm[at + t] for t in range(touch))
            for o, d in peers:
                copy2(o, d).start()

        add(first_tile(jnp.maximum(i - 2, 0)))
        weigh(first_tile(jnp.clip(i - 1, 0, count - 1)))
        measure(first_tile(jnp.minimum(i, count - 1)))
        return carry

    lax.fori_loop(0, count + 2, body, 0)
    for s in range(slots):
        ret[1, me * slots + s] = back[1, me * slots + s]

    loads["send_v"].wait()
    loads["touch_v"].wait()
    loads["pair_v"].wait()
    used = 2 * pairs + (touch + 1) * recv_count
    rows = -(-used // 128) * 128
    index = jnp.concatenate(
        [pair_v[0:1], pair_v[1:2]]
        + [touch_v[t : t + 1] for t in range(touch)]
        + [send_v[o, s : s + 1] for o in range(3) for s in range(slots)]
        + [jnp.full((1, rows - used), -1, jnp.int32)],
        axis=1,
    )
    here = lax.broadcasted_iota(jnp.int32, (blocks, rows), 0)
    pick = jnp.where(here == index, 1.0, 0.0).astype(BF16)
    for o, d in peers:
        arrival(ret, recv2, o, d)

    def plane(k):
        found = [aterm[0:pairs, k, :], bterm[0:pairs, k, :]]
        found += [aterm[pl.ds(pairs + t, recv_count, touch), k, :] for t in range(touch)]
        if slots == 1:
            found += [ret[o, :, k, :] for o in range(3)]
        else:
            found += [
                ret[o, pl.ds(s, nbulk, slots), k, :] for o in range(3) for s in range(slots)
            ]
        return jnp.concatenate(found + [jnp.zeros((rows - used, width), F32)], axis=0)

    totals = []
    for k in range(4):
        parts = split3(plane(k))
        totals.append(
            sum(jnp.dot(pick, part.astype(BF16), preferred_element_type=F32) for part in parts)
        )
    loads["vel"].wait()
    loads["sto"].wait()
    for k in range(3):
        speed = vel_ref[k] + time_step * totals[k]
        nv_ref[k] = speed
        nf_ref[:, k, :] = fld_ref[:, k, :] + time_step * speed
    nf_ref[:, 3, :] = fld_ref[:, 3, :] + time_step * totals[3] / sto_ref[...]

    loads["move_s"].wait()
    for d in range(nbulk):
        for m in range(mig):
            entry = move_s[m, 0, d]
            at = jnp.maximum(entry, 0)
            live = entry >= 0
            slot = d * mig + m
            mstage[slot, 0:4] = jnp.where(live, nf_ref[at], 0.0)
            for k in range(3):
                mstage[slot, 4 + k : 5 + k] = jnp.where(live, nv_ref[k, pl.ds(at, 1), :], 0.0)
                mstage[slot, 7 + k : 8 + k] = jnp.where(live, pos_ref[k, pl.ds(at, 1), :], 0.0)
            mstage[slot, 10:11] = jnp.where(live, sto_ref[pl.ds(at, 1), :], 0.0)
            mstage[slot, 11:16] = jnp.zeros((5, width), F32)
    others = [lax.rem(me + step, nbulk) for step in range(1, nbulk)]
    for d in others:
        copy3(d).start()
    for m in range(mig):
        mgot[me * mig + m] = mstage[me * mig + m]
    for o, d in peers:
        copy1(o, d).wait_send()
        copy2(o, d).wait_send()
    for d in others:
        landed = mgot.at[pl.ds(d * mig, mig)]
        pltpu.make_async_copy(landed, landed, recv3.at[d]).wait()
    for k in range(11):
        arr_ref[k] = mgot[:, k, :]
    for d in others:
        copy3(d).wait_send()


def solution(mesh):
    nreg, nbulk = mesh.shape["region"], mesh.shape["bulk"]

    def per_device(
        positions,
        fields,
        storage,
        velocity,
        send_list,
        remote_local,
        remote_mask,
        local_pairs,
        local_mask,
        migrate_list,
    ):
        blocks, _, width = positions.shape
        slots = send_list.shape[3]
        recv_count, touch = remote_local.shape[1:]
        pairs = local_pairs.shape[1]
        mig = migrate_list.shape[2]
        per = nbulk * slots
        tiles = pairs + touch * recv_count
        held = blocks + recv_count
        sends = send_list[0].transpose(0, 2, 1)
        touches = remote_local[0].T
        pair_rows = local_pairs[0].T
        moves = migrate_list[0].T[:, None, :]
        vmem = pl.BlockSpec(memory_space=pltpu.VMEM)
        dma = pltpu.SemaphoreType.DMA
        new_fields, speed, arrived = pl.pallas_call(
            functools.partial(kernel, nreg, nbulk),
            out_shape=(
                jax.ShapeDtypeStruct((blocks, 4, width), F32),
                jax.ShapeDtypeStruct((3, blocks, width), F32),
                jax.ShapeDtypeStruct((11, nbulk * mig, width), F32),
            ),
            in_specs=[pl.BlockSpec(memory_space=pltpu.HBM)] * 10,
            out_specs=(vmem, vmem, vmem),
            scratch_shapes=[
                pltpu.VMEM((3, blocks, width), F32),
                pltpu.VMEM((blocks, 4, width), F32),
                pltpu.VMEM((blocks, width), F32),
                pltpu.VMEM((3, blocks, width), F32),
                pltpu.SMEM(sends.shape, jnp.int32),
                pltpu.SMEM(touches.shape, jnp.int32),
                pltpu.SMEM(pair_rows.shape, jnp.int32),
                pltpu.SMEM(moves.shape, jnp.int32),
                pltpu.VMEM(sends.shape, jnp.int32),
                pltpu.VMEM(touches.shape, jnp.int32),
                pltpu.VMEM(pair_rows.shape, jnp.int32),
                pltpu.VMEM((tiles,) + local_mask.shape[2:], jnp.int32),
                pltpu.VMEM((held, 8, width), F32),
                pltpu.VMEM((3, per, 8, width), F32),
                pltpu.VMEM((3, per, 8, width), F32),
                pltpu.VMEM((3, per, 8, width), F32),
                pltpu.VMEM((3, per, 8, width), F32),
                pltpu.VMEM((nbulk * mig, 16, width), F32),
                pltpu.VMEM((nbulk * mig, 16, width), F32),
                pltpu.VMEM((held, 48, width), BF16),
                pltpu.VMEM((blocks, 48, width), BF16),
                pltpu.VMEM((held, 16, 2 * width), BF16),
                pltpu.SMEM((2, tiles), jnp.int32),
                pltpu.VMEM((tiles, 8, width), F32),
                pltpu.VMEM((tiles, 8, width), F32),
                pltpu.VMEM((LANES // 2, width, 2 * width), F32),
                pltpu.VMEM((LANES // 2, 2, 2 * width, 2 * width), BF16),
                dma((13,)),
                dma((3, nbulk)),
                dma((3, nbulk)),
                dma((3, nbulk)),
                dma((3, nbulk)),
                dma((nbulk,)),
                dma((nbulk,)),
            ],
            compiler_params=pltpu.CompilerParams(
                collective_id=0, has_side_effects=True, vmem_limit_bytes=64 << 20
            ),
        )(
            positions.transpose(1, 0, 2),
            fields,
            storage,
            velocity.transpose(1, 0, 2),
            sends,
            touches,
            pair_rows,
            moves,
            remote_mask[0].reshape((touch * recv_count,) + remote_mask.shape[3:]),
            local_mask[0],
        )
        return new_fields, speed.transpose(1, 0, 2), arrived.transpose(1, 0, 2)

    both = ("region", "bulk")
    return jax.shard_map(
        per_device,
        mesh=mesh,
        in_specs=(
            P(both, None, None),
            P(both, None, None),
            P(both, None),
            P(both, None, None),
            P(both, None, None, None),
            P(both, None, None),
            P(both, None, None, None, None),
            P(both, None, None),
            P(both, None, None, None),
            P(both, None, None),
        ),
        out_specs=(
            P(both, None, None),
            P(both, None, None),
            P(both, None, None),
        ),
        check_vma=False,
    )
```

```python
import functools

import jax
import jax.numpy as jnp
from jax import lax
from jax.experimental import pallas as pl
from jax.experimental.pallas import tpu as pltpu
from jax.sharding import PartitionSpec as P

MESH = pl.DeviceIdType.MESH
bond_stiff = 0.1
leak_gain = 0.5
time_step = 0.5
half_press = 0.025
LANES = 8
PACK = 4
F32 = jnp.float32
BF16 = jnp.bfloat16


def rows_of(shape):
    return lax.broadcasted_iota(jnp.int32, shape, len(shape) - 2)


def roll(x, by):
    return pltpu.roll(x, by % 8, x.ndim - 2)


def top(x):
    return x.astype(BF16).astype(F32)


def split3(x):
    first = top(x)
    rest = x - first
    second = top(rest)
    return first, second, rest - second


def features(block):
    row = rows_of(block.shape)
    half = jnp.where(row < 3, 0.5 * block, 0.0)
    norm = jnp.sum(half * half, axis=-2, keepdims=True) + 0.5
    h1, h2, h3 = split3(half)
    n1, n2, n3 = split3(norm)

    def eight(first, second, second_last, last):
        return jnp.where(
            row < 6, first + roll(second, 3), jnp.where(row == 6, second_last, last)
        )

    blank = jnp.zeros_like(half)
    b_rows = [eight(h1, h1, n1, 1.0), eight(h2, h2, n2, 1.0), eight(h1, h3, n3, 1.0), blank]
    a_rows = [
        eight(-2.0 * h1, -2.0 * h2, 1.0, n1),
        eight(-2.0 * h1, -2.0 * h2, 1.0, n2),
        eight(-2.0 * h3, -2.0 * h1, 1.0, n3),
        blank,
    ]
    flat = jnp.concatenate(b_rows, axis=-2).reshape(-1, PACK * 32, block.shape[-1])
    left = jnp.stack([flat[n].T for n in range(flat.shape[0])]).astype(BF16)
    right = jnp.concatenate(a_rows, axis=-2).astype(BF16)
    press = block[..., 6:7, :]
    moved = roll(block, -3)
    product = -0.25 * press * block
    product_top = top(product)
    moved_top = top(moved)
    block_top = top(block)
    press_top = top(press)
    spring_0 = jnp.where(row < 3, moved_top, jnp.where(row == 3, 1.0, 0.0))
    spring_1 = jnp.where((row >= 1) & (row < 4), roll(moved - moved_top, 1), 0.0)
    leak_0 = jnp.where(
        row < 3,
        product_top,
        jnp.where(
            row == 3, 0.0, jnp.where(row == 4, 1.0, jnp.where(row == 5, press_top, roll(block_top, 6)))
        ),
    )
    leak_1 = jnp.where(
        row == 0,
        roll(block_top, 6),
        jnp.where(
            row < 4,
            roll(product - product_top, 1),
            jnp.where(row == 4, press - press_top, roll(block - block_top, 5)),
        ),
    )
    sums = jnp.concatenate(
        [
            jnp.concatenate([spring_0, spring_1], axis=-2),
            jnp.concatenate([leak_0, leak_1], axis=-2),
        ],
        axis=-1,
    ).astype(BF16)
    return left, right, sums


def combine(block, out):
    row = rows_of(block.shape)
    r0, r1 = out[:8], out[8:]
    o1 = r0 + roll(r1, -1)
    o2 = r0[3:4]
    o4 = r0[4:5]
    o5 = r0[5:6] + r1[4:5]
    o3 = jnp.where(row < 2, roll(r0, 2), roll(r1, 2)) + roll(r1, 3)
    press = block[6:7]
    force = bond_stiff * (o1 - roll(block, -3) * o2) + half_press * (
        block * (press * o4 + o5) - press * o3
    )
    leak = leak_gain * (o5 - press * o4)
    return jnp.where(row < 3, force, jnp.where(row == 3, leak, 0.0))


ALONG_J = (((1,), (0,)), ((), ()))
ALONG_I = (((1,), (1,)), ((), ()))
dot = functools.partial(lax.dot_general, preferred_element_type=F32)


def distance(left_b, right_a, part):
    spread = [jnp.where(part == k, right_a, jnp.zeros_like(right_a)) for k in range(PACK)]
    return dot(left_b, jnp.concatenate(spread, axis=0), ALONG_J)


def split_weights(dist, packed):
    guess = pl.reciprocal(dist, approx=True)
    weight = guess * (2.0 - dist * guess)
    words, width = packed.shape
    bit = lax.shift_left(1, rows_of((1, 8, width)))
    intact = (jnp.broadcast_to(packed[:, None, :], (words, 8, width)) & bit) != 0
    intact = intact.reshape(words * 8, width)
    spring = jnp.where(intact, weight, 0.0)
    leak = jnp.where(intact, 0.0, weight)
    spring_hi = spring.astype(BF16)
    leak_hi = leak.astype(BF16)
    spring_lo = (spring - spring_hi.astype(F32)).astype(BF16)
    leak_lo = (leak - leak_hi.astype(F32)).astype(BF16)
    return spring_hi, leak_hi, spring_lo, leak_lo


def kernel(
    nreg,
    nbulk,
    pos_hbm,
    fld_hbm,
    sto_hbm,
    vel_hbm,
    send_hbm,
    touch_hbm,
    pair_hbm,
    move_hbm,
    rmask_hbm,
    lmask_hbm,
    nf_ref,
    nv_ref,
    arr_ref,
    pos_ref,
    fld_ref,
    sto_ref,
    vel_ref,
    send_s,
    touch_s,
    pair_s,
    move_s,
    send_v,
    touch_v,
    pair_v,
    masks,
    pts,
    stage,
    got,
    back,
    ret,
    mstage,
    mgot,
    left,
    right,
    sums,
    tab,
    aterm,
    bterm,
    dists,
    weights,
    load_sem,
    send1,
    recv1,
    send2,
    recv2,
    send3,
    recv3,
):
    blocks, width = sto_ref.shape
    slots = send_s.shape[1]
    per = nbulk * slots
    recv_count = 3 * per
    pairs = pair_s.shape[1]
    touch = touch_s.shape[0]
    mig = move_s.shape[0]
    r = lax.axis_index("region")
    me = lax.axis_index("bulk")

    def region_at(by):
        return lax.rem(r + by + nreg, nreg)

    peers = []
    for o in (0, 2, 1):
        for step in range(nbulk):
            if o == 1 and step == 0:
                continue
            peers.append((o, lax.rem(me + step, nbulk)))

    loads = {}
    for n, (name, src, dst) in enumerate(
        (
            ("send_s", send_hbm, send_s),
            ("pos", pos_hbm, pos_ref),
            ("fld", fld_hbm, fld_ref),
            ("pair_s", pair_hbm, pair_s),
            ("lmask", lmask_hbm, masks.at[pl.ds(0, pairs)]),
            ("touch_s", touch_hbm, touch_s),
            ("rmask", rmask_hbm, masks.at[pl.ds(pairs, touch * recv_count)]),
            ("vel", vel_hbm, vel_ref),
            ("sto", sto_hbm, sto_ref),
            ("move_s", move_hbm, move_s),
            ("send_v", send_hbm, send_v),
            ("touch_v", touch_hbm, touch_v),
            ("pair_v", pair_hbm, pair_v),
        )
    ):
        loads[name] = pltpu.make_async_copy(src, dst, load_sem.at[n])
        loads[name].start()

    barrier = pltpu.get_barrier_semaphore()
    for o, d in peers:
        pl.semaphore_signal(barrier, inc=1, device_id=(region_at(o - 1), d), device_id_type=MESH)

    loads["pos"].wait()
    loads["fld"].wait()
    for k in range(3):
        pts[0:blocks, k, :] = pos_ref[k]
    for k in range(4):
        pts[0:blocks, 3 + k, :] = fld_ref[:, k, :]
    pts[0:blocks, 7, :] = jnp.zeros((blocks, width), F32)
    loads["send_s"].wait()
    for o in range(3):
        for s in range(slots):
            for d in range(nbulk):
                stage[o, d * slots + s] = pts[send_s[o, s, d]]
    for s in range(slots):
        got[1, me * slots + s] = stage[1, me * slots + s]

    def span(ref, o, d):
        return ref.at[o, pl.ds(d * slots, slots)]

    def copy1(o, d):
        return pltpu.make_async_remote_copy(
            src_ref=span(stage, o, d),
            dst_ref=span(got, o, me),
            send_sem=send1.at[o, d],
            recv_sem=recv1.at[o, me],
            device_id=(region_at(o - 1), d),
            device_id_type=MESH,
        )

    def copy2(o, b):
        return pltpu.make_async_remote_copy(
            src_ref=span(back, o, b),
            dst_ref=span(ret, o, me),
            send_sem=send2.at[o, b],
            recv_sem=recv2.at[o, me],
            device_id=(region_at(1 - o), b),
            device_id_type=MESH,
        )

    def copy3(d):
        return pltpu.make_async_remote_copy(
            src_ref=mstage.at[pl.ds(d * mig, mig)],
            dst_ref=mgot.at[pl.ds(me * mig, mig)],
            send_sem=send3.at[d],
            recv_sem=recv3.at[me],
            device_id=(r, d),
            device_id_type=MESH,
        )

    def arrival(ref, sem, o, b):
        pltpu.make_async_copy(span(ref, o, b), span(ref, o, b), sem.at[o, b]).wait()

    pl.semaphore_wait(barrier, len(peers))
    for o, d in peers:
        copy1(o, d).start()

    group = 8

    def build(step, carry):
        at = pl.ds(step * group, group)
        packs = pl.ds(step * (group // PACK), group // PACK)
        left[packs], right[at], sums[at] = features(pts[at])
        return carry

    lax.fori_loop(0, blocks // group, build, 0)

    loads["pair_s"].wait()
    loads["touch_s"].wait()
    for t in range(pairs):
        tab[0, t] = pair_s[0, t]
        tab[1, t] = pair_s[1, t]
    for q in range(recv_count):
        for t in range(touch):
            tab[0, pairs + touch * q + t] = touch_s[t, q]
            tab[1, pairs + touch * q + t] = blocks + q
    loads["lmask"].wait()
    loads["rmask"].wait()

    local_groups = pairs // LANES
    remote_groups = touch * recv_count // LANES
    count = local_groups + remote_groups
    early = local_groups // 2
    begin = early
    done = early + remote_groups

    def first_tile(i):
        shifted = jnp.where(
            i < begin, i, jnp.where(i < done, i + (local_groups - early), i - remote_groups)
        )
        return LANES * shifted

    def measure(first):
        for u in range(LANES):
            b = tab[1, first + u]
            dists[u] = distance(left[lax.div(b, PACK)], right[tab[0, first + u]], lax.rem(b, PACK))

    def weigh(first):
        for u in range(LANES):
            s_hi, l_hi, s_lo, l_lo = split_weights(dists[u], masks[first + u])
            weights[u, 0, 0:width] = s_hi
            weights[u, 0, width:] = l_hi
            weights[u, 1, 0:width] = s_lo
            weights[u, 1, width:] = l_lo

    def add(first):
        for u in range(LANES):
            a = tab[0, first + u]
            b = tab[1, first + u]
            on_a = on_b = None
            for piece in range(2):
                w = weights[u, piece]
                turned = jnp.concatenate([w[:width], w[width:]], axis=1)
                part_a = dot(sums[b], w, ALONG_J)
                part_b = dot(sums[a], turned, ALONG_I)
                on_a = part_a if on_a is None else on_a + part_a
                on_b = part_b if on_b is None else on_b + part_b
            aterm[first + u] = combine(pts[a], on_a)
            bterm[first + u] = combine(pts[b], on_b)

    def body(i, carry):
        @pl.when(i == begin)
        def _():
            for o, d in peers:
                arrival(got, recv1, o, d)
            for o in range(3):
                for step in range(per // group):
                    block = got[o, step * group : (step + 1) * group]
                    to = pl.ds(blocks + o * per + step * group, group)
                    pts[to] = block
                    packs = pl.ds((blocks + o * per + step * group) // PACK, group // PACK)
                    left[packs], _, sums[to] = features(block)

        @pl.when(i == done + 2)
        def _():
            for o in range(3):
                for s in range(per):
                    at = pairs + touch * (o * per + s)
                    back[o, s] = sum(bterm[at + t] for t in range(touch))
            for o, d in peers:
                copy2(o, d).start()

        add(first_tile(jnp.maximum(i - 2, 0)))
        weigh(first_tile(jnp.clip(i - 1, 0, count - 1)))
        measure(first_tile(jnp.minimum(i, count - 1)))
        return carry

    lax.fori_loop(0, count + 2, body, 0)
    for s in range(slots):
        ret[1, me * slots + s] = back[1, me * slots + s]

    loads["send_v"].wait()
    loads["touch_v"].wait()
    loads["pair_v"].wait()
    used = 2 * pairs + (touch + 1) * recv_count
    rows = -(-used // 128) * 128
    index = jnp.concatenate(
        [pair_v[0:1], pair_v[1:2]]
        + [touch_v[t : t + 1] for t in range(touch)]
        + [send_v[o, s : s + 1] for o in range(3) for s in range(slots)]
        + [jnp.full((1, rows - used), -1, jnp.int32)],
        axis=1,
    )
    here = lax.broadcasted_iota(jnp.int32, (blocks, rows), 0)
    pick = jnp.where(here == index, 1.0, 0.0).astype(BF16)
    for o, d in peers:
        arrival(ret, recv2, o, d)

    def plane(k):
        found = [aterm[0:pairs, k, :], bterm[0:pairs, k, :]]
        found += [aterm[pl.ds(pairs + t, recv_count, touch), k, :] for t in range(touch)]
        if slots == 1:
            found += [ret[o, :, k, :] for o in range(3)]
        else:
            found += [
                ret[o, pl.ds(s, nbulk, slots), k, :] for o in range(3) for s in range(slots)
            ]
        return jnp.concatenate(found + [jnp.zeros((rows - used, width), F32)], axis=0)

    totals = []
    for k in range(4):
        parts = split3(plane(k))
        totals.append(
            sum(jnp.dot(pick, part.astype(BF16), preferred_element_type=F32) for part in parts)
        )
    loads["vel"].wait()
    loads["sto"].wait()
    for k in range(3):
        speed = vel_ref[k] + time_step * totals[k]
        nv_ref[k] = speed
        nf_ref[:, k, :] = fld_ref[:, k, :] + time_step * speed
    nf_ref[:, 3, :] = fld_ref[:, 3, :] + time_step * totals[3] / sto_ref[...]

    loads["move_s"].wait()
    for d in range(nbulk):
        for m in range(mig):
            entry = move_s[m, 0, d]
            at = jnp.maximum(entry, 0)
            live = entry >= 0
            slot = d * mig + m
            mstage[slot, 0:4] = jnp.where(live, nf_ref[at], 0.0)
            for k in range(3):
                mstage[slot, 4 + k : 5 + k] = jnp.where(live, nv_ref[k, pl.ds(at, 1), :], 0.0)
                mstage[slot, 7 + k : 8 + k] = jnp.where(live, pos_ref[k, pl.ds(at, 1), :], 0.0)
            mstage[slot, 10:11] = jnp.where(live, sto_ref[pl.ds(at, 1), :], 0.0)
            mstage[slot, 11:16] = jnp.zeros((5, width), F32)
    others = [lax.rem(me + step, nbulk) for step in range(1, nbulk)]
    for d in others:
        copy3(d).start()
    for m in range(mig):
        mgot[me * mig + m] = mstage[me * mig + m]
    for o, d in peers:
        copy1(o, d).wait_send()
        copy2(o, d).wait_send()
    for d in others:
        landed = mgot.at[pl.ds(d * mig, mig)]
        pltpu.make_async_copy(landed, landed, recv3.at[d]).wait()
    for k in range(11):
        arr_ref[k] = mgot[:, k, :]
    for d in others:
        copy3(d).wait_send()


def solution(mesh):
    nreg, nbulk = mesh.shape["region"], mesh.shape["bulk"]

    def per_device(
        positions,
        fields,
        storage,
        velocity,
        send_list,
        remote_local,
        remote_mask,
        local_pairs,
        local_mask,
        migrate_list,
    ):
        blocks, _, width = positions.shape
        slots = send_list.shape[3]
        recv_count, touch = remote_local.shape[1:]
        pairs = local_pairs.shape[1]
        mig = migrate_list.shape[2]
        per = nbulk * slots
        tiles = pairs + touch * recv_count
        held = blocks + recv_count
        sends = send_list[0].transpose(0, 2, 1)
        touches = remote_local[0].T
        pair_rows = local_pairs[0].T
        moves = migrate_list[0].T[:, None, :]
        vmem = pl.BlockSpec(memory_space=pltpu.VMEM)
        dma = pltpu.SemaphoreType.DMA
        new_fields, speed, arrived = pl.pallas_call(
            functools.partial(kernel, nreg, nbulk),
            out_shape=(
                jax.ShapeDtypeStruct((blocks, 4, width), F32),
                jax.ShapeDtypeStruct((3, blocks, width), F32),
                jax.ShapeDtypeStruct((11, nbulk * mig, width), F32),
            ),
            in_specs=[pl.BlockSpec(memory_space=pltpu.HBM)] * 10,
            out_specs=(vmem, vmem, vmem),
            scratch_shapes=[
                pltpu.VMEM((3, blocks, width), F32),
                pltpu.VMEM((blocks, 4, width), F32),
                pltpu.VMEM((blocks, width), F32),
                pltpu.VMEM((3, blocks, width), F32),
                pltpu.SMEM(sends.shape, jnp.int32),
                pltpu.SMEM(touches.shape, jnp.int32),
                pltpu.SMEM(pair_rows.shape, jnp.int32),
                pltpu.SMEM(moves.shape, jnp.int32),
                pltpu.VMEM(sends.shape, jnp.int32),
                pltpu.VMEM(touches.shape, jnp.int32),
                pltpu.VMEM(pair_rows.shape, jnp.int32),
                pltpu.VMEM((tiles,) + local_mask.shape[2:], jnp.int32),
                pltpu.VMEM((held, 8, width), F32),
                pltpu.VMEM((3, per, 8, width), F32),
                pltpu.VMEM((3, per, 8, width), F32),
                pltpu.VMEM((3, per, 8, width), F32),
                pltpu.VMEM((3, per, 8, width), F32),
                pltpu.VMEM((nbulk * mig, 16, width), F32),
                pltpu.VMEM((nbulk * mig, 16, width), F32),
                pltpu.VMEM((held // PACK, width, PACK * 32), BF16),
                pltpu.VMEM((blocks, 32, width), BF16),
                pltpu.VMEM((held, 16, 2 * width), BF16),
                pltpu.SMEM((2, tiles), jnp.int32),
                pltpu.VMEM((tiles, 8, width), F32),
                pltpu.VMEM((tiles, 8, width), F32),
                pltpu.VMEM((LANES, width, width), F32),
                pltpu.VMEM((LANES, 2, 2 * width, width), BF16),
                dma((13,)),
                dma((3, nbulk)),
                dma((3, nbulk)),
                dma((3, nbulk)),
                dma((3, nbulk)),
                dma((nbulk,)),
                dma((nbulk,)),
            ],
            compiler_params=pltpu.CompilerParams(
                collective_id=0, has_side_effects=True, vmem_limit_bytes=64 << 20
            ),
        )(
            positions.transpose(1, 0, 2),
            fields,
            storage,
            velocity.transpose(1, 0, 2),
            sends,
            touches,
            pair_rows,
            moves,
            remote_mask[0].reshape((touch * recv_count,) + remote_mask.shape[3:]),
            local_mask[0],
        )
        return new_fields, speed.transpose(1, 0, 2), arrived.transpose(1, 0, 2)

    both = ("region", "bulk")
    return jax.shard_map(
        per_device,
        mesh=mesh,
        in_specs=(
            P(both, None, None),
            P(both, None, None),
            P(both, None),
            P(both, None, None),
            P(both, None, None, None),
            P(both, None, None),
            P(both, None, None, None, None),
            P(both, None, None),
            P(both, None, None, None),
            P(both, None, None),
        ),
        out_specs=(
            P(both, None, None),
            P(both, None, None),
            P(both, None, None),
        ),
        check_vma=False,
    )
```

```python
import functools

import jax
import jax.numpy as jnp
from jax import lax
from jax.experimental import pallas as pl
from jax.experimental.pallas import tpu as pltpu
from jax.sharding import PartitionSpec as P

MESH = pl.DeviceIdType.MESH
bond_stiff = 0.1
leak_gain = 0.5
time_step = 0.5
half_press = 0.025
LANES = 8
PACK = 4
F32 = jnp.float32
BF16 = jnp.bfloat16


def rows_of(shape):
    return lax.broadcasted_iota(jnp.int32, shape, len(shape) - 2)


def roll(x, by):
    return pltpu.roll(x, by % 8, x.ndim - 2)


def top(x):
    return x.astype(BF16).astype(F32)


def split3(x):
    first = top(x)
    rest = x - first
    second = top(rest)
    return first, second, rest - second


def features(block):
    row = rows_of(block.shape)
    half = jnp.where(row < 3, 0.5 * block, 0.0)
    norm = jnp.sum(half * half, axis=-2, keepdims=True) + 0.5
    h1, h2, h3 = split3(half)
    n1, n2, n3 = split3(norm)

    def eight(first, second, second_last, last):
        return jnp.where(
            row < 6, first + roll(second, 3), jnp.where(row == 6, second_last, last)
        )

    blank = jnp.zeros_like(half)
    b_rows = [eight(h1, h1, n1, 1.0), eight(h2, h2, n2, 1.0), eight(h1, h3, n3, 1.0), blank]
    a_rows = [
        eight(-2.0 * h1, -2.0 * h2, 1.0, n1),
        eight(-2.0 * h1, -2.0 * h2, 1.0, n2),
        eight(-2.0 * h3, -2.0 * h1, 1.0, n3),
        blank,
    ]
    flat = jnp.concatenate(b_rows, axis=-2).reshape(-1, PACK * 32, block.shape[-1])
    left = jnp.stack([flat[n].T for n in range(flat.shape[0])]).astype(BF16)
    right = jnp.concatenate(a_rows, axis=-2).astype(BF16)
    press = block[..., 6:7, :]
    moved = roll(block, -3)
    product = -0.25 * press * block
    product_top = top(product)
    moved_top = top(moved)
    block_top = top(block)
    press_top = top(press)
    spring_0 = jnp.where(row < 3, moved_top, jnp.where(row == 3, 1.0, 0.0))
    spring_1 = jnp.where((row >= 1) & (row < 4), roll(moved - moved_top, 1), 0.0)
    leak_0 = jnp.where(
        row < 3,
        product_top,
        jnp.where(
            row == 3, 0.0, jnp.where(row == 4, 1.0, jnp.where(row == 5, press_top, roll(block_top, 6)))
        ),
    )
    leak_1 = jnp.where(
        row == 0,
        roll(block_top, 6),
        jnp.where(
            row < 4,
            roll(product - product_top, 1),
            jnp.where(row == 4, press - press_top, roll(block - block_top, 5)),
        ),
    )
    sums = jnp.concatenate(
        [
            jnp.concatenate([spring_0, spring_1], axis=-2),
            jnp.concatenate([leak_0, leak_1], axis=-2),
        ],
        axis=-1,
    ).astype(BF16)
    return left, right, sums


def combine(block, out):
    row = rows_of(block.shape)
    r0, r1 = out[:8], out[8:]
    o1 = r0 + roll(r1, -1)
    o2 = r0[3:4]
    o4 = r0[4:5]
    o5 = r0[5:6] + r1[4:5]
    o3 = jnp.where(row < 2, roll(r0, 2), roll(r1, 2)) + roll(r1, 3)
    press = block[6:7]
    force = bond_stiff * (o1 - roll(block, -3) * o2) + half_press * (
        block * (press * o4 + o5) - press * o3
    )
    leak = leak_gain * (o5 - press * o4)
    return jnp.where(row < 3, force, jnp.where(row == 3, leak, 0.0))


ALONG_J = (((1,), (0,)), ((), ()))
ALONG_I = (((1,), (1,)), ((), ()))
dot = functools.partial(lax.dot_general, preferred_element_type=F32)


def distance(left_b, right_a, part):
    spread = [jnp.where(part == k, right_a, jnp.zeros_like(right_a)) for k in range(PACK)]
    return dot(left_b, jnp.concatenate(spread, axis=0), ALONG_J)


def split_weights(dist, packed):
    guess = pl.reciprocal(dist, approx=True)
    weight = guess * (2.0 - dist * guess)
    words, width = packed.shape
    bit = lax.shift_left(1, rows_of((1, 8, width)))
    intact = (jnp.broadcast_to(packed[:, None, :], (words, 8, width)) & bit) != 0
    intact = intact.reshape(words * 8, width)
    spring = jnp.where(intact, weight, 0.0)
    leak = jnp.where(intact, 0.0, weight)
    spring_hi = spring.astype(BF16)
    leak_hi = leak.astype(BF16)
    spring_lo = (spring - spring_hi.astype(F32)).astype(BF16)
    leak_lo = (leak - leak_hi.astype(F32)).astype(BF16)
    return spring_hi, leak_hi, spring_lo, leak_lo


def kernel(
    nreg,
    nbulk,
    pos_hbm,
    fld_hbm,
    sto_hbm,
    vel_hbm,
    send_hbm,
    touch_hbm,
    pair_hbm,
    move_hbm,
    rmask_hbm,
    lmask_hbm,
    nf_hbm,
    nv_hbm,
    arr_hbm,
    nf_ref,
    nv_ref,
    arr_ref,
    pos_ref,
    fld_ref,
    sto_ref,
    vel_ref,
    send_s,
    touch_s,
    pair_s,
    move_s,
    send_v,
    touch_v,
    pair_v,
    masks,
    pts,
    stage,
    got,
    back,
    ret,
    mstage,
    mgot,
    left,
    right,
    sums,
    terms,
    bterm,
    dists,
    weights,
    load_sem,
    out_sem,
    send1,
    recv1,
    send2,
    recv2,
    send3,
    recv3,
):
    blocks, width = sto_ref.shape
    slots = send_s.shape[1]
    per = nbulk * slots
    recv_count = 3 * per
    pairs = pair_s.shape[1]
    touch = touch_s.shape[0]
    mig = move_s.shape[0]
    r = lax.axis_index("region")
    me = lax.axis_index("bulk")

    def region_at(by):
        return lax.rem(r + by + nreg, nreg)

    peers = []
    for o in (0, 2, 1):
        for step in range(nbulk):
            if o == 1 and step == 0:
                continue
            peers.append((o, lax.rem(me + step, nbulk)))

    barrier = pltpu.get_barrier_semaphore()
    for o, d in peers:
        pl.semaphore_signal(barrier, inc=1, device_id=(region_at(o - 1), d), device_id_type=MESH)

    loads = {}
    for n, (name, src, dst) in enumerate(
        (
            ("send_s", send_hbm, send_s),
            ("pos", pos_hbm, pos_ref),
            ("fld", fld_hbm, fld_ref),
            ("pair_s", pair_hbm, pair_s),
            ("lmask", lmask_hbm, masks.at[pl.ds(0, pairs)]),
            ("touch_s", touch_hbm, touch_s),
            ("rmask", rmask_hbm, masks.at[pl.ds(pairs, touch * recv_count)]),
            ("vel", vel_hbm, vel_ref),
            ("sto", sto_hbm, sto_ref),
            ("move_s", move_hbm, move_s),
            ("send_v", send_hbm, send_v),
            ("touch_v", touch_hbm, touch_v),
            ("pair_v", pair_hbm, pair_v),
        )
    ):
        loads[name] = pltpu.make_async_copy(src, dst, load_sem.at[n])
        loads[name].start()

    loads["pos"].wait()
    loads["fld"].wait()
    for k in range(3):
        pts[0:blocks, k, :] = pos_ref[k]
    for k in range(4):
        pts[0:blocks, 3 + k, :] = fld_ref[:, k, :]
    pts[0:blocks, 7, :] = jnp.zeros((blocks, width), F32)
    loads["send_s"].wait()
    for o in range(3):
        for s in range(slots):
            for d in range(nbulk):
                stage[o, d * slots + s] = pts[send_s[o, s, d]]
    for s in range(slots):
        got[1, me * slots + s] = stage[1, me * slots + s]

    def span(ref, o, d):
        return ref.at[o, pl.ds(d * slots, slots)]

    def copy1(o, d):
        return pltpu.make_async_remote_copy(
            src_ref=span(stage, o, d),
            dst_ref=span(got, o, me),
            send_sem=send1.at[o, d],
            recv_sem=recv1.at[o, me],
            device_id=(region_at(o - 1), d),
            device_id_type=MESH,
        )

    def copy2(o, b):
        return pltpu.make_async_remote_copy(
            src_ref=span(back, o, b),
            dst_ref=span(ret, o, me),
            send_sem=send2.at[o, b],
            recv_sem=recv2.at[o, me],
            device_id=(region_at(1 - o), b),
            device_id_type=MESH,
        )

    def copy3(d):
        return pltpu.make_async_remote_copy(
            src_ref=mstage.at[pl.ds(d * mig, mig)],
            dst_ref=mgot.at[pl.ds(me * mig, mig)],
            send_sem=send3.at[d],
            recv_sem=recv3.at[me],
            device_id=(r, d),
            device_id_type=MESH,
        )

    def arrival(ref, sem, o, b):
        pltpu.make_async_copy(span(ref, o, b), span(ref, o, b), sem.at[o, b]).wait()

    group = 8

    def build(step, carry):
        at = pl.ds(step * group, group)
        packs = pl.ds(step * (group // PACK), group // PACK)
        left[packs], right[at], sums[at] = features(pts[at])
        return carry

    lax.fori_loop(0, blocks // group, build, 0)

    pl.semaphore_wait(barrier, len(peers))
    for o, d in peers:
        copy1(o, d).start()

    loads["pair_s"].wait()
    loads["touch_s"].wait()
    loads["lmask"].wait()
    loads["rmask"].wait()

    local_groups = pairs // LANES
    remote_groups = touch * recv_count // LANES
    count = local_groups + remote_groups
    early = local_groups // 2
    begin = early
    done = early + remote_groups

    def first_tile(i):
        shifted = jnp.where(
            i < begin, i, jnp.where(i < done, i + (local_groups - early), i - remote_groups)
        )
        return LANES * shifted

    tiles = pairs + touch * recv_count

    def members(first):
        remote = first >= pairs
        near = jnp.minimum(first, pairs - LANES)
        far = jnp.maximum(first - pairs, 0)
        t = far // recv_count
        q = far % recv_count
        found = []
        for u in range(LANES):
            found.append(
                (
                    jnp.where(remote, touch_s[t, q + u], pair_s[0, near + u]),
                    jnp.where(remote, blocks + q + u, pair_s[1, near + u]),
                    jnp.where(remote, pairs + touch * (q + u) + t, near + u),
                    first + u,
                )
            )
        return found

    def measure(first):
        for u, (a, b, _, _) in enumerate(members(first)):
            dists[u] = distance(left[lax.div(b, PACK)], right[a], lax.rem(b, PACK))

    def weigh(first):
        for u, (_, _, m, _) in enumerate(members(first)):
            s_hi, l_hi, s_lo, l_lo = split_weights(dists[u], masks[m])
            weights[u, 0, 0:width] = s_hi
            weights[u, 0, width:] = l_hi
            weights[u, 1, 0:width] = s_lo
            weights[u, 1, width:] = l_lo

    def put(at, value):
        terms[:, pl.ds(at, 1), :] = value[0:4].reshape(4, 1, width)

    def add(first):
        for u, (a, b, _, n) in enumerate(members(first)):
            on_a = on_b = None
            for piece in range(2):
                w = weights[u, piece]
                turned = jnp.concatenate([w[:width], w[width:]], axis=1)
                part_a = dot(sums[b], w, ALONG_J)
                part_b = dot(sums[a], turned, ALONG_I)
                on_a = part_a if on_a is None else on_a + part_a
                on_b = part_b if on_b is None else on_b + part_b
            put(n, combine(pts[a], on_a))
            term = combine(pts[b], on_b)
            put(tiles + n, term)
            bterm[n] = term

    def body(i, carry):
        @pl.when(i == begin)
        def _():
            for o, d in peers:
                arrival(got, recv1, o, d)
            for o in range(3):
                for step in range(per // group):
                    block = got[o, step * group : (step + 1) * group]
                    to = pl.ds(blocks + o * per + step * group, group)
                    pts[to] = block
                    packs = pl.ds((blocks + o * per + step * group) // PACK, group // PACK)
                    left[packs], _, sums[to] = features(block)

        @pl.when(i == done + 2)
        def _():
            for o in range(3):
                for s in range(per):
                    at = pairs + o * per + s
                    back[o, s] = sum(bterm[at + t * recv_count] for t in range(touch))
            for o, d in peers:
                copy2(o, d).start()

        add(first_tile(jnp.maximum(i - 2, 0)))
        weigh(first_tile(jnp.clip(i - 1, 0, count - 1)))
        measure(first_tile(jnp.minimum(i, count - 1)))
        return carry

    lax.fori_loop(0, count + 2, body, 0)
    for s in range(slots):
        ret[1, me * slots + s] = back[1, me * slots + s]

    loads["send_v"].wait()
    loads["touch_v"].wait()
    loads["pair_v"].wait()
    used = 2 * tiles + recv_count
    rows = terms.shape[1]

    def none(n):
        return jnp.full((1, n), -1, jnp.int32)

    index = jnp.concatenate(
        [pair_v[0:1]]
        + [touch_v[t : t + 1] for t in range(touch)]
        + [pair_v[1:2], none(touch * recv_count)]
        + [send_v[o, s : s + 1] for o in range(3) for s in range(slots)]
        + [none(rows - used)],
        axis=1,
    )
    here = lax.broadcasted_iota(jnp.int32, (blocks, rows), 0)
    pick = jnp.where(here == index, 1.0, 0.0).astype(BF16)
    for o, d in peers:
        arrival(ret, recv2, o, d)

    for o in range(3):
        for s in range(slots):
            for d in range(nbulk):
                put(2 * tiles + (o * slots + s) * nbulk + d, ret[o, d * slots + s])
    terms[:, used:, :] = jnp.zeros((4, rows - used, width), F32)
    totals = []
    for k in range(4):
        parts = split3(terms[k])
        totals.append(
            sum(jnp.dot(pick, part.astype(BF16), preferred_element_type=F32) for part in parts)
        )
    loads["vel"].wait()
    loads["sto"].wait()
    for k in range(3):
        speed = vel_ref[k] + time_step * totals[k]
        nv_ref[k] = speed
        nf_ref[:, k, :] = fld_ref[:, k, :] + time_step * speed
    nf_ref[:, 3, :] = fld_ref[:, 3, :] + time_step * totals[3] / sto_ref[...]

    outs = [
        pltpu.make_async_copy(src, dst, out_sem.at[n])
        for n, (src, dst) in enumerate(
            ((nf_ref, nf_hbm), (nv_ref, nv_hbm), (arr_ref, arr_hbm))
        )
    ]
    outs[0].start()
    outs[1].start()
    loads["move_s"].wait()
    for d in range(nbulk):
        for m in range(mig):
            entry = move_s[m, 0, d]
            at = jnp.maximum(entry, 0)
            live = entry >= 0
            slot = d * mig + m
            mstage[slot, 0:4] = jnp.where(live, nf_ref[at], 0.0)
            for k in range(3):
                mstage[slot, 4 + k : 5 + k] = jnp.where(live, nv_ref[k, pl.ds(at, 1), :], 0.0)
                mstage[slot, 7 + k : 8 + k] = jnp.where(live, pos_ref[k, pl.ds(at, 1), :], 0.0)
            mstage[slot, 10:11] = jnp.where(live, sto_ref[pl.ds(at, 1), :], 0.0)
            mstage[slot, 11:16] = jnp.zeros((5, width), F32)
    others = [lax.rem(me + step, nbulk) for step in range(1, nbulk)]
    for d in others:
        copy3(d).start()
    for m in range(mig):
        mgot[me * mig + m] = mstage[me * mig + m]
    for o, d in peers:
        copy1(o, d).wait_send()
        copy2(o, d).wait_send()
    for d in others:
        landed = mgot.at[pl.ds(d * mig, mig)]
        pltpu.make_async_copy(landed, landed, recv3.at[d]).wait()
    for k in range(11):
        arr_ref[k] = mgot[:, k, :]
    outs[2].start()
    for d in others:
        copy3(d).wait_send()
    for out in outs:
        out.wait()


def hand_out(*refs):
    sems = refs[6]
    copies = [pltpu.make_async_copy(refs[n], refs[3 + n], sems.at[n]) for n in range(3)]
    for copy in copies:
        copy.start()
    for copy in copies:
        copy.wait()


def solution(mesh):
    nreg, nbulk = mesh.shape["region"], mesh.shape["bulk"]

    def per_device(
        positions,
        fields,
        storage,
        velocity,
        send_list,
        remote_local,
        remote_mask,
        local_pairs,
        local_mask,
        migrate_list,
    ):
        blocks, _, width = positions.shape
        slots = send_list.shape[3]
        recv_count, touch = remote_local.shape[1:]
        pairs = local_pairs.shape[1]
        mig = migrate_list.shape[2]
        per = nbulk * slots
        tiles = pairs + touch * recv_count
        held = blocks + recv_count
        rows = -(-(2 * tiles + recv_count) // 128) * 128
        sends = send_list[0].transpose(0, 2, 1)
        touches = remote_local[0].T
        pair_rows = local_pairs[0].T
        moves = migrate_list[0].T[:, None, :]
        hbm = pl.BlockSpec(memory_space=pltpu.HBM)
        out_shape = (
            jax.ShapeDtypeStruct((blocks, 4, width), F32),
            jax.ShapeDtypeStruct((3, blocks, width), F32),
            jax.ShapeDtypeStruct((11, nbulk * mig, width), F32),
        )
        dma = pltpu.SemaphoreType.DMA
        results = pl.pallas_call(
            functools.partial(kernel, nreg, nbulk),
            out_shape=out_shape,
            in_specs=[hbm] * 10,
            out_specs=(hbm, hbm, hbm),
            scratch_shapes=[
                pltpu.VMEM((blocks, 4, width), F32),
                pltpu.VMEM((3, blocks, width), F32),
                pltpu.VMEM((11, nbulk * mig, width), F32),
                pltpu.VMEM((3, blocks, width), F32),
                pltpu.VMEM((blocks, 4, width), F32),
                pltpu.VMEM((blocks, width), F32),
                pltpu.VMEM((3, blocks, width), F32),
                pltpu.SMEM(sends.shape, jnp.int32),
                pltpu.SMEM(touches.shape, jnp.int32),
                pltpu.SMEM(pair_rows.shape, jnp.int32),
                pltpu.SMEM(moves.shape, jnp.int32),
                pltpu.VMEM(sends.shape, jnp.int32),
                pltpu.VMEM(touches.shape, jnp.int32),
                pltpu.VMEM(pair_rows.shape, jnp.int32),
                pltpu.VMEM((tiles,) + local_mask.shape[2:], jnp.int32),
                pltpu.VMEM((held, 8, width), F32),
                pltpu.VMEM((3, per, 8, width), F32),
                pltpu.VMEM((3, per, 8, width), F32),
                pltpu.VMEM((3, per, 8, width), F32),
                pltpu.VMEM((3, per, 8, width), F32),
                pltpu.VMEM((nbulk * mig, 16, width), F32),
                pltpu.VMEM((nbulk * mig, 16, width), F32),
                pltpu.VMEM((held // PACK, width, PACK * 32), BF16),
                pltpu.VMEM((blocks, 32, width), BF16),
                pltpu.VMEM((held, 16, 2 * width), BF16),
                pltpu.VMEM((4, rows, width), F32),
                pltpu.VMEM((tiles, 8, width), F32),
                pltpu.VMEM((LANES, width, width), F32),
                pltpu.VMEM((LANES, 2, 2 * width, width), BF16),
                dma((13,)),
                dma((3,)),
                dma((3, nbulk)),
                dma((3, nbulk)),
                dma((3, nbulk)),
                dma((3, nbulk)),
                dma((nbulk,)),
                dma((nbulk,)),
            ],
            compiler_params=pltpu.CompilerParams(
                collective_id=0, has_side_effects=True, vmem_limit_bytes=64 << 20
            ),
        )(
            positions.transpose(1, 0, 2),
            fields,
            storage,
            velocity.transpose(1, 0, 2),
            sends,
            touches,
            pair_rows,
            moves,
            remote_mask[0].reshape((touch * recv_count,) + remote_mask.shape[3:]),
            local_mask[0],
        )
        new_fields, speed, arrived = pl.pallas_call(
            hand_out,
            out_shape=out_shape,
            in_specs=[hbm] * 3,
            out_specs=(hbm, hbm, hbm),
            scratch_shapes=[dma((3,))],
            compiler_params=pltpu.CompilerParams(vmem_limit_bytes=64 << 20),
        )(*results)
        return new_fields, speed.transpose(1, 0, 2), arrived.transpose(1, 0, 2)

    both = ("region", "bulk")
    return jax.shard_map(
        per_device,
        mesh=mesh,
        in_specs=(
            P(both, None, None),
            P(both, None, None),
            P(both, None),
            P(both, None, None),
            P(both, None, None, None),
            P(both, None, None),
            P(both, None, None, None, None),
            P(both, None, None),
            P(both, None, None, None),
            P(both, None, None),
        ),
        out_specs=(
            P(both, None, None),
            P(both, None, None),
            P(both, None, None),
        ),
        check_vma=False,
    )
```

```python
import functools

import jax
import jax.numpy as jnp
from jax import lax
from jax.experimental import pallas as pl
from jax.experimental.pallas import tpu as pltpu
from jax.sharding import PartitionSpec as P

MESH = pl.DeviceIdType.MESH
bond_stiff = 0.1
leak_gain = 0.5
time_step = 0.5
half_press = 0.025
LANES = 4
PACK = 4
F32 = jnp.float32
BF16 = jnp.bfloat16


def rows_of(shape):
    return lax.broadcasted_iota(jnp.int32, shape, len(shape) - 2)


def roll(x, by):
    return pltpu.roll(x, by % 8, x.ndim - 2)


def top(x):
    return x.astype(BF16).astype(F32)


def split3(x):
    first = top(x)
    rest = x - first
    second = top(rest)
    return first, second, rest - second


def features(block):
    row = rows_of(block.shape)
    half = jnp.where(row < 3, 0.5 * block, 0.0)
    norm = jnp.sum(half * half, axis=-2, keepdims=True) + 0.5
    h1, h2, h3 = split3(half)
    n1, n2, n3 = split3(norm)

    def eight(first, second, second_last, last):
        return jnp.where(
            row < 6, first + roll(second, 3), jnp.where(row == 6, second_last, last)
        )

    blank = jnp.zeros_like(half)
    b_rows = [eight(h1, h1, n1, 1.0), eight(h2, h2, n2, 1.0), eight(h1, h3, n3, 1.0), blank]
    a_rows = [
        eight(-2.0 * h1, -2.0 * h2, 1.0, n1),
        eight(-2.0 * h1, -2.0 * h2, 1.0, n2),
        eight(-2.0 * h3, -2.0 * h1, 1.0, n3),
        blank,
    ]
    flat = jnp.concatenate(b_rows, axis=-2).reshape(-1, PACK * 32, block.shape[-1])
    turned = [flat[n].T.astype(BF16) for n in range(flat.shape[0])]
    left = jnp.stack([t[:, 32 * m : 32 * m + 32] for t in turned for m in range(PACK)])
    right = jnp.concatenate(a_rows, axis=-2).astype(BF16)
    press = block[..., 6:7, :]
    moved = roll(block, -3)
    product = -0.25 * press * block
    product_top = top(product)
    moved_top = top(moved)
    block_top = top(block)
    press_top = top(press)
    spring_0 = jnp.where(row < 3, moved_top, jnp.where(row == 3, 1.0, 0.0))
    spring_1 = jnp.where((row >= 1) & (row < 4), roll(moved - moved_top, 1), 0.0)
    leak_0 = jnp.where(
        row < 3,
        product_top,
        jnp.where(
            row == 3, 0.0, jnp.where(row == 4, 1.0, jnp.where(row == 5, press_top, roll(block_top, 6)))
        ),
    )
    leak_1 = jnp.where(
        row == 0,
        roll(block_top, 6),
        jnp.where(
            row < 4,
            roll(product - product_top, 1),
            jnp.where(row == 4, press - press_top, roll(block - block_top, 5)),
        ),
    )
    sums = jnp.concatenate(
        [
            jnp.concatenate([spring_0, spring_1], axis=-2),
            jnp.concatenate([leak_0, leak_1], axis=-2),
        ],
        axis=-1,
    ).astype(BF16)
    return left, right, sums


def combine(block, out):
    row = rows_of(block.shape)
    r0, r1 = out[:8], out[8:]
    o1 = r0 + roll(r1, -1)
    o2 = r0[3:4]
    o4 = r0[4:5]
    o5 = r0[5:6] + r1[4:5]
    o3 = jnp.where(row < 2, roll(r0, 2), roll(r1, 2)) + roll(r1, 3)
    press = block[6:7]
    force = bond_stiff * (o1 - roll(block, -3) * o2) + half_press * (
        block * (press * o4 + o5) - press * o3
    )
    leak = leak_gain * (o5 - press * o4)
    return jnp.where(row < 3, force, jnp.where(row == 3, leak, 0.0))


ALONG_J = (((1,), (0,)), ((), ()))
ALONG_I = (((1,), (1,)), ((), ()))
dot = functools.partial(lax.dot_general, preferred_element_type=F32)


def distance(left_b, right_a):
    return dot(left_b, right_a, ALONG_J)


def split_weights(dist, packed):
    guess = pl.reciprocal(dist, approx=True)
    weight = guess * (2.0 - dist * guess)
    words, width = packed.shape
    bit = lax.shift_left(1, rows_of((1, 8, width)))
    intact = (jnp.broadcast_to(packed[:, None, :], (words, 8, width)) & bit) != 0
    intact = intact.reshape(words * 8, width)
    spring = jnp.where(intact, weight, 0.0)
    leak = jnp.where(intact, 0.0, weight)
    spring_hi = spring.astype(BF16)
    leak_hi = leak.astype(BF16)
    spring_lo = (spring - spring_hi.astype(F32)).astype(BF16)
    leak_lo = (leak - leak_hi.astype(F32)).astype(BF16)
    return spring_hi, leak_hi, spring_lo, leak_lo


def kernel(
    nreg,
    nbulk,
    pos_hbm,
    fld_hbm,
    sto_hbm,
    vel_hbm,
    send_hbm,
    touch_hbm,
    pair_hbm,
    move_hbm,
    rmask_hbm,
    lmask_hbm,
    nf_hbm,
    nv_hbm,
    arr_hbm,
    nf_ref,
    nv_ref,
    arr_ref,
    pos_ref,
    fld_ref,
    sto_ref,
    vel_ref,
    send_s,
    touch_s,
    pair_s,
    move_s,
    send_v,
    touch_v,
    pair_v,
    masks,
    pts,
    stage,
    got,
    back,
    ret,
    mstage,
    mgot,
    left,
    right,
    sums,
    terms,
    bterm,
    dists,
    weights,
    load_sem,
    out_sem,
    send1,
    recv1,
    send2,
    recv2,
    send3,
    recv3,
):
    blocks, width = sto_ref.shape
    slots = send_s.shape[1]
    per = nbulk * slots
    recv_count = 3 * per
    pairs = pair_s.shape[1]
    touch = touch_s.shape[0]
    mig = move_s.shape[0]
    r = lax.axis_index("region")
    me = lax.axis_index("bulk")

    def region_at(by):
        return lax.rem(r + by + nreg, nreg)

    peers = []
    for o in (0, 2, 1):
        for step in range(nbulk):
            if o == 1 and step == 0:
                continue
            peers.append((o, lax.rem(me + step, nbulk)))

    barrier = pltpu.get_barrier_semaphore()
    for o, d in peers:
        pl.semaphore_signal(barrier, inc=1, device_id=(region_at(o - 1), d), device_id_type=MESH)

    loads = {}
    for n, (name, src, dst) in enumerate(
        (
            ("send_s", send_hbm, send_s),
            ("pos", pos_hbm, pos_ref),
            ("fld", fld_hbm, fld_ref),
            ("pair_s", pair_hbm, pair_s),
            ("lmask", lmask_hbm, masks.at[pl.ds(0, pairs)]),
            ("touch_s", touch_hbm, touch_s),
            ("rmask", rmask_hbm, masks.at[pl.ds(pairs, touch * recv_count)]),
            ("vel", vel_hbm, vel_ref),
            ("sto", sto_hbm, sto_ref),
            ("move_s", move_hbm, move_s),
            ("send_v", send_hbm, send_v),
            ("touch_v", touch_hbm, touch_v),
            ("pair_v", pair_hbm, pair_v),
        )
    ):
        loads[name] = pltpu.make_async_copy(src, dst, load_sem.at[n])
        loads[name].start()

    loads["pos"].wait()
    loads["fld"].wait()
    for k in range(3):
        pts[0:blocks, k, :] = pos_ref[k]
    for k in range(4):
        pts[0:blocks, 3 + k, :] = fld_ref[:, k, :]
    pts[0:blocks, 7, :] = jnp.zeros((blocks, width), F32)
    loads["send_s"].wait()
    for o in range(3):
        for s in range(slots):
            for d in range(nbulk):
                stage[o * per + d * slots + s] = pts[send_s[o, s, d]]
    for s in range(slots):
        got[per + me * slots + s] = stage[per + me * slots + s]

    def span(ref, o, d):
        return ref.at[pl.ds(o * per + d * slots, slots)]

    def copy1(o, d):
        return pltpu.make_async_remote_copy(
            src_ref=span(stage, o, d),
            dst_ref=span(got, o, me),
            send_sem=send1,
            recv_sem=recv1,
            device_id=(region_at(o - 1), d),
            device_id_type=MESH,
        )

    def copy2(o, b):
        return pltpu.make_async_remote_copy(
            src_ref=span(back, o, b),
            dst_ref=span(ret, o, me),
            send_sem=send2,
            recv_sem=recv2,
            device_id=(region_at(1 - o), b),
            device_id_type=MESH,
        )

    def copy3(d):
        return pltpu.make_async_remote_copy(
            src_ref=mstage.at[pl.ds(d * mig, mig)],
            dst_ref=mgot.at[pl.ds(me * mig, mig)],
            send_sem=send3,
            recv_sem=recv3,
            device_id=(r, d),
            device_id_type=MESH,
        )

    def await_all(ref, count, sem):
        whole = ref.at[pl.ds(0, count)]
        pltpu.make_async_copy(whole, whole, sem).wait()

    group = 8

    def build(step, carry):
        at = pl.ds(step * group, group)
        left[at], right[at], sums[at] = features(pts[at])
        return carry

    lax.fori_loop(0, blocks // group, build, 0)

    pl.semaphore_wait(barrier, len(peers))
    for o, d in peers:
        copy1(o, d).start()

    loads["pair_s"].wait()
    loads["touch_s"].wait()
    loads["lmask"].wait()
    loads["rmask"].wait()

    local_groups = pairs // LANES
    remote_groups = touch * recv_count // LANES
    count = local_groups + remote_groups
    early = local_groups // 2
    begin = early
    done = early + remote_groups

    def first_tile(i):
        shifted = jnp.where(
            i < begin, i, jnp.where(i < done, i + (local_groups - early), i - remote_groups)
        )
        return LANES * shifted

    tiles = pairs + touch * recv_count

    def members(first):
        remote = first >= pairs
        near = jnp.minimum(first, pairs - LANES)
        far = jnp.maximum(first - pairs, 0)
        t = far // recv_count
        q = far % recv_count
        found = []
        for u in range(LANES):
            found.append(
                (
                    jnp.where(remote, touch_s[t, q + u], pair_s[0, near + u]),
                    jnp.where(remote, blocks + q + u, pair_s[1, near + u]),
                    jnp.where(remote, pairs + touch * (q + u) + t, near + u),
                    first + u,
                )
            )
        return found

    def measure(first):
        for u, (a, b, _, _) in enumerate(members(first)):
            dists[u] = distance(left[b], right[a])

    def weigh(first):
        for u, (_, _, m, _) in enumerate(members(first)):
            s_hi, l_hi, s_lo, l_lo = split_weights(dists[u], masks[m])
            weights[u, 0, 0:width] = s_hi
            weights[u, 0, width:] = l_hi
            weights[u, 1, 0:width] = s_lo
            weights[u, 1, width:] = l_lo

    def put(at, value):
        terms[:, pl.ds(at, 1), :] = value[0:4].reshape(4, 1, width)

    def add(first):
        for u, (a, b, _, n) in enumerate(members(first)):
            on_a = on_b = None
            for piece in range(2):
                w = weights[u, piece]
                turned = jnp.concatenate([w[:width], w[width:]], axis=1)
                part_a = dot(sums[b], w, ALONG_J)
                part_b = dot(sums[a], turned, ALONG_I)
                on_a = part_a if on_a is None else on_a + part_a
                on_b = part_b if on_b is None else on_b + part_b
            put(n, combine(pts[a], on_a))
            term = combine(pts[b], on_b)
            put(tiles + n, term)
            bterm[n] = term

    def body(i, carry):
        @pl.when(i == begin)
        def _():
            await_all(got, len(peers) * slots, recv1)
            for step in range(recv_count // group):
                block = got[step * group : (step + 1) * group]
                to = pl.ds(blocks + step * group, group)
                pts[to] = block
                left[to], _, sums[to] = features(block)

        @pl.when(i == done + 2)
        def _():
            for o in range(3):
                for s in range(per):
                    at = pairs + o * per + s
                    back[o * per + s] = sum(bterm[at + t * recv_count] for t in range(touch))
            for o, d in peers:
                copy2(o, d).start()

        add(first_tile(jnp.maximum(i - 2, 0)))
        weigh(first_tile(jnp.clip(i - 1, 0, count - 1)))
        measure(first_tile(jnp.minimum(i, count - 1)))
        return carry

    lax.fori_loop(0, count + 2, body, 0)
    for s in range(slots):
        ret[per + me * slots + s] = back[per + me * slots + s]

    loads["send_v"].wait()
    loads["touch_v"].wait()
    loads["pair_v"].wait()
    used = 2 * tiles + recv_count
    rows = terms.shape[1]

    def none(n):
        return jnp.full((1, n), -1, jnp.int32)

    index = jnp.concatenate(
        [pair_v[0:1]]
        + [touch_v[t : t + 1] for t in range(touch)]
        + [pair_v[1:2], none(touch * recv_count)]
        + [send_v[o, s : s + 1] for o in range(3) for s in range(slots)]
        + [none(rows - used)],
        axis=1,
    )
    here = lax.broadcasted_iota(jnp.int32, (blocks, rows), 0)
    pick = jnp.where(here == index, 1.0, 0.0).astype(BF16)
    await_all(ret, len(peers) * slots, recv2)

    for o in range(3):
        for s in range(slots):
            for d in range(nbulk):
                put(2 * tiles + (o * slots + s) * nbulk + d, ret[o * per + d * slots + s])
    terms[:, used:, :] = jnp.zeros((4, rows - used, width), F32)
    totals = []
    for k in range(4):
        parts = split3(terms[k])
        totals.append(
            sum(jnp.dot(pick, part.astype(BF16), preferred_element_type=F32) for part in parts)
        )
    loads["vel"].wait()
    loads["sto"].wait()
    for k in range(3):
        speed = vel_ref[k] + time_step * totals[k]
        nv_ref[k] = speed
        nf_ref[:, k, :] = fld_ref[:, k, :] + time_step * speed
    nf_ref[:, 3, :] = fld_ref[:, 3, :] + time_step * totals[3] / sto_ref[...]

    outs = [
        pltpu.make_async_copy(src, dst, out_sem.at[n])
        for n, (src, dst) in enumerate(
            ((nf_ref, nf_hbm), (nv_ref, nv_hbm), (arr_ref, arr_hbm))
        )
    ]
    outs[0].start()
    outs[1].start()
    loads["move_s"].wait()
    for d in range(nbulk):
        for m in range(mig):
            entry = move_s[m, 0, d]
            at = jnp.maximum(entry, 0)
            live = entry >= 0
            slot = d * mig + m
            mstage[slot, 0:4] = jnp.where(live, nf_ref[at], 0.0)
            for k in range(3):
                mstage[slot, 4 + k : 5 + k] = jnp.where(live, nv_ref[k, pl.ds(at, 1), :], 0.0)
                mstage[slot, 7 + k : 8 + k] = jnp.where(live, pos_ref[k, pl.ds(at, 1), :], 0.0)
            mstage[slot, 10:11] = jnp.where(live, sto_ref[pl.ds(at, 1), :], 0.0)
            mstage[slot, 11:16] = jnp.zeros((5, width), F32)
    others = [lax.rem(me + step, nbulk) for step in range(1, nbulk)]
    for d in others:
        copy3(d).start()
    for m in range(mig):
        mgot[me * mig + m] = mstage[me * mig + m]
    await_all(stage, len(peers) * slots, send1)
    await_all(back, len(peers) * slots, send2)
    await_all(mgot, len(others) * mig, recv3)
    for k in range(11):
        arr_ref[k] = mgot[:, k, :]
    outs[2].start()
    await_all(mstage, len(others) * mig, send3)
    for out in outs:
        out.wait()


def hand_out(*refs):
    sems = refs[9]
    into = [pltpu.make_async_copy(refs[n], refs[6 + n], sems.at[n]) for n in range(3)]
    out = [pltpu.make_async_copy(refs[6 + n], refs[3 + n], sems.at[3 + n]) for n in range(3)]
    for copy in into:
        copy.start()
    for n in range(3):
        into[n].wait()
        out[n].start()
    for copy in out:
        copy.wait()


def solution(mesh):
    nreg, nbulk = mesh.shape["region"], mesh.shape["bulk"]

    def per_device(
        positions,
        fields,
        storage,
        velocity,
        send_list,
        remote_local,
        remote_mask,
        local_pairs,
        local_mask,
        migrate_list,
    ):
        blocks, _, width = positions.shape
        slots = send_list.shape[3]
        recv_count, touch = remote_local.shape[1:]
        pairs = local_pairs.shape[1]
        mig = migrate_list.shape[2]
        per = nbulk * slots
        tiles = pairs + touch * recv_count
        held = blocks + recv_count
        rows = -(-(2 * tiles + recv_count) // 128) * 128
        sends = send_list[0].transpose(0, 2, 1)
        touches = remote_local[0].T
        pair_rows = local_pairs[0].T
        moves = migrate_list[0].T[:, None, :]
        hbm = pl.BlockSpec(memory_space=pltpu.HBM)
        out_shape = (
            jax.ShapeDtypeStruct((blocks, 4, width), F32),
            jax.ShapeDtypeStruct((3, blocks, width), F32),
            jax.ShapeDtypeStruct((11, nbulk * mig, width), F32),
        )
        dma = pltpu.SemaphoreType.DMA
        results = pl.pallas_call(
            functools.partial(kernel, nreg, nbulk),
            out_shape=out_shape,
            in_specs=[hbm] * 10,
            out_specs=(hbm, hbm, hbm),
            scratch_shapes=[
                pltpu.VMEM((blocks, 4, width), F32),
                pltpu.VMEM((3, blocks, width), F32),
                pltpu.VMEM((11, nbulk * mig, width), F32),
                pltpu.VMEM((3, blocks, width), F32),
                pltpu.VMEM((blocks, 4, width), F32),
                pltpu.VMEM((blocks, width), F32),
                pltpu.VMEM((3, blocks, width), F32),
                pltpu.SMEM(sends.shape, jnp.int32),
                pltpu.SMEM(touches.shape, jnp.int32),
                pltpu.SMEM(pair_rows.shape, jnp.int32),
                pltpu.SMEM(moves.shape, jnp.int32),
                pltpu.VMEM(sends.shape, jnp.int32),
                pltpu.VMEM(touches.shape, jnp.int32),
                pltpu.VMEM(pair_rows.shape, jnp.int32),
                pltpu.VMEM((tiles,) + local_mask.shape[2:], jnp.int32),
                pltpu.VMEM((held, 8, width), F32),
                pltpu.VMEM((recv_count, 8, width), F32),
                pltpu.VMEM((recv_count, 8, width), F32),
                pltpu.VMEM((recv_count, 8, width), F32),
                pltpu.VMEM((recv_count, 8, width), F32),
                pltpu.VMEM((nbulk * mig, 16, width), F32),
                pltpu.VMEM((nbulk * mig, 16, width), F32),
                pltpu.VMEM((held, width, 32), BF16),
                pltpu.VMEM((blocks, 32, width), BF16),
                pltpu.VMEM((held, 16, 2 * width), BF16),
                pltpu.VMEM((4, rows, width), F32),
                pltpu.VMEM((tiles, 8, width), F32),
                pltpu.VMEM((LANES, width, width), F32),
                pltpu.VMEM((LANES, 2, 2 * width, width), BF16),
                dma((13,)),
                dma((3,)),
                dma,
                dma,
                dma,
                dma,
                dma,
                dma,
            ],
            compiler_params=pltpu.CompilerParams(
                collective_id=0, has_side_effects=True, vmem_limit_bytes=64 << 20
            ),
        )(
            positions.transpose(1, 0, 2),
            fields,
            storage,
            velocity.transpose(1, 0, 2),
            sends,
            touches,
            pair_rows,
            moves,
            remote_mask[0].reshape((touch * recv_count,) + remote_mask.shape[3:]),
            local_mask[0],
        )
        new_fields, speed, arrived = pl.pallas_call(
            hand_out,
            out_shape=out_shape,
            in_specs=[hbm] * 3,
            out_specs=(hbm, hbm, hbm),
            scratch_shapes=[pltpu.VMEM(o.shape, F32) for o in out_shape] + [dma((6,))],
            compiler_params=pltpu.CompilerParams(vmem_limit_bytes=64 << 20),
        )(*results)
        return new_fields, speed.transpose(1, 0, 2), arrived.transpose(1, 0, 2)

    both = ("region", "bulk")
    return jax.shard_map(
        per_device,
        mesh=mesh,
        in_specs=(
            P(both, None, None),
            P(both, None, None),
            P(both, None),
            P(both, None, None),
            P(both, None, None, None),
            P(both, None, None),
            P(both, None, None, None, None),
            P(both, None, None),
            P(both, None, None, None),
            P(both, None, None),
        ),
        out_specs=(
            P(both, None, None),
            P(both, None, None),
            P(both, None, None),
        ),
        check_vma=False,
    )
```

```python
import functools

import jax
import jax.numpy as jnp
from jax import lax
from jax.experimental import pallas as pl
from jax.experimental.pallas import tpu as pltpu
from jax.sharding import PartitionSpec as P

MESH = pl.DeviceIdType.MESH
bond_stiff = 0.1
leak_gain = 0.5
time_step = 0.5
half_press = 0.025
LANES = 4
PACK = 4
F32 = jnp.float32
BF16 = jnp.bfloat16


def rows_of(shape):
    return lax.broadcasted_iota(jnp.int32, shape, len(shape) - 2)


def roll(x, by):
    return pltpu.roll(x, by % 8, x.ndim - 2)


def top(x):
    return x.astype(BF16).astype(F32)


def split3(x):
    first = top(x)
    rest = x - first
    second = top(rest)
    return first, second, rest - second


def features(block):
    row = rows_of(block.shape)
    half = jnp.where(row < 3, 0.5 * block, 0.0)
    norm = jnp.sum(half * half, axis=-2, keepdims=True) + 0.5
    h1, h2, h3 = split3(half)
    n1, n2, n3 = split3(norm)

    def eight(first, second, second_last, last):
        return jnp.where(
            row < 6, first + roll(second, 3), jnp.where(row == 6, second_last, last)
        )

    blank = jnp.zeros_like(half)
    b_rows = [eight(h1, h1, n1, 1.0), eight(h2, h2, n2, 1.0), eight(h1, h3, n3, 1.0), blank]
    a_rows = [
        eight(-2.0 * h1, -2.0 * h2, 1.0, n1),
        eight(-2.0 * h1, -2.0 * h2, 1.0, n2),
        eight(-2.0 * h3, -2.0 * h1, 1.0, n3),
        blank,
    ]
    flat = jnp.concatenate(b_rows, axis=-2).reshape(-1, PACK * 32, block.shape[-1])
    turned = [flat[n].T.astype(BF16) for n in range(flat.shape[0])]
    left = jnp.stack([t[:, 32 * m : 32 * m + 32] for t in turned for m in range(PACK)])
    right = jnp.concatenate(a_rows, axis=-2).astype(BF16)
    press = block[..., 6:7, :]
    moved = roll(block, -3)
    product = -0.25 * press * block
    product_top = top(product)
    moved_top = top(moved)
    block_top = top(block)
    press_top = top(press)
    spring_0 = jnp.where(row < 3, moved_top, jnp.where(row == 3, 1.0, 0.0))
    spring_1 = jnp.where((row >= 1) & (row < 4), roll(moved - moved_top, 1), 0.0)
    leak_0 = jnp.where(
        row < 3,
        product_top,
        jnp.where(
            row == 3, 0.0, jnp.where(row == 4, 1.0, jnp.where(row == 5, press_top, roll(block_top, 6)))
        ),
    )
    leak_1 = jnp.where(
        row == 0,
        roll(block_top, 6),
        jnp.where(
            row < 4,
            roll(product - product_top, 1),
            jnp.where(row == 4, press - press_top, roll(block - block_top, 5)),
        ),
    )
    sums = jnp.concatenate(
        [
            jnp.concatenate([spring_0, spring_1], axis=-2),
            jnp.concatenate([leak_0, leak_1], axis=-2),
        ],
        axis=-1,
    ).astype(BF16)
    return left, right, sums


def combine(block, out):
    row = rows_of(block.shape)
    r0, r1 = out[:8], out[8:]
    o1 = r0 + roll(r1, -1)
    o2 = r0[3:4]
    o4 = r0[4:5]
    o5 = r0[5:6] + r1[4:5]
    o3 = jnp.where(row < 2, roll(r0, 2), roll(r1, 2)) + roll(r1, 3)
    press = block[6:7]
    force = bond_stiff * (o1 - roll(block, -3) * o2) + half_press * (
        block * (press * o4 + o5) - press * o3
    )
    leak = leak_gain * (o5 - press * o4)
    return jnp.where(row < 3, force, jnp.where(row == 3, leak, 0.0))


ALONG_J = (((1,), (0,)), ((), ()))
ALONG_I = (((1,), (1,)), ((), ()))
dot = functools.partial(lax.dot_general, preferred_element_type=F32)


def distance(left_b, right_a):
    return dot(left_b, right_a, ALONG_J)


def split_weights(dist, packed):
    guess = pl.reciprocal(dist, approx=True)
    weight = guess * (2.0 - dist * guess)
    words, width = packed.shape
    bit = lax.shift_left(1, rows_of((1, 8, width)))
    intact = (jnp.broadcast_to(packed[:, None, :], (words, 8, width)) & bit) != 0
    intact = intact.reshape(words * 8, width)
    spring = jnp.where(intact, weight, 0.0)
    leak = jnp.where(intact, 0.0, weight)
    spring_hi = spring.astype(BF16)
    leak_hi = leak.astype(BF16)
    spring_lo = (spring - spring_hi.astype(F32)).astype(BF16)
    leak_lo = (leak - leak_hi.astype(F32)).astype(BF16)
    return spring_hi, leak_hi, spring_lo, leak_lo


def kernel(
    nreg,
    nbulk,
    pos_hbm,
    fld_hbm,
    sto_hbm,
    vel_hbm,
    send_hbm,
    touch_hbm,
    pair_hbm,
    move_hbm,
    rmask_hbm,
    lmask_hbm,
    nf_hbm,
    nv_hbm,
    arr_hbm,
    nf_ref,
    nv_ref,
    arr_ref,
    pos_ref,
    fld_ref,
    sto_ref,
    vel_ref,
    send_s,
    touch_s,
    pair_s,
    move_s,
    send_v,
    touch_v,
    pair_v,
    masks,
    pts,
    stage,
    got,
    back,
    ret,
    mstage,
    mgot,
    left,
    right,
    sums,
    terms,
    bterm,
    dists,
    weights,
    load_sem,
    out_sem,
    send1,
    recv1,
    send2,
    recv2,
    send3,
    recv3,
):
    blocks, width = sto_ref.shape
    slots = send_s.shape[1]
    per = nbulk * slots
    recv_count = 3 * per
    pairs = pair_s.shape[1]
    touch = touch_s.shape[0]
    mig = move_s.shape[0]
    r = lax.axis_index("region")
    me = lax.axis_index("bulk")

    def region_at(by):
        return lax.rem(r + by + nreg, nreg)

    peers = []
    for o in range(3):
        for step in range(nbulk):
            if o == 1 and step == 0:
                continue
            peers.append((o, lax.rem(me + step, nbulk)))

    barrier = pltpu.get_barrier_semaphore()
    for o, d in peers:
        pl.semaphore_signal(barrier, inc=1, device_id=(region_at(o - 1), d), device_id_type=MESH)

    loads = {}
    for n, (name, src, dst) in enumerate(
        (
            ("send_s", send_hbm, send_s),
            ("pos", pos_hbm, pos_ref),
            ("fld", fld_hbm, fld_ref),
            ("pair_s", pair_hbm, pair_s),
            ("lmask", lmask_hbm, masks.at[pl.ds(0, pairs)]),
            ("touch_s", touch_hbm, touch_s),
            ("rmask", rmask_hbm, masks.at[pl.ds(pairs, touch * recv_count)]),
            ("vel", vel_hbm, vel_ref),
            ("sto", sto_hbm, sto_ref),
            ("move_s", move_hbm, move_s),
            ("send_v", send_hbm, send_v),
            ("touch_v", touch_hbm, touch_v),
            ("pair_v", pair_hbm, pair_v),
        )
    ):
        loads[name] = pltpu.make_async_copy(src, dst, load_sem.at[n])
        loads[name].start()

    loads["pos"].wait()
    loads["fld"].wait()
    for k in range(3):
        pts[0:blocks, k, :] = pos_ref[k]
    for k in range(4):
        pts[0:blocks, 3 + k, :] = fld_ref[:, k, :]
    pts[0:blocks, 7, :] = jnp.zeros((blocks, width), F32)
    loads["send_s"].wait()
    for o in range(3):
        for s in range(slots):
            for d in range(nbulk):
                stage[o * per + d * slots + s] = pts[send_s[o, s, d]]
    for s in range(slots):
        got[per + me * slots + s] = stage[per + me * slots + s]

    def span(ref, o, d):
        return ref.at[pl.ds(o * per + d * slots, slots)]

    def copy1(o, d):
        return pltpu.make_async_remote_copy(
            src_ref=span(stage, o, d),
            dst_ref=span(got, o, me),
            send_sem=send1,
            recv_sem=recv1.at[o],
            device_id=(region_at(o - 1), d),
            device_id_type=MESH,
        )

    def copy2(q):
        o = q // per
        b = q % per // slots
        s = q % slots
        return pltpu.make_async_remote_copy(
            src_ref=back.at[pl.ds(q, 1)],
            dst_ref=ret.at[pl.ds(o * per + me * slots + s, 1)],
            send_sem=send2,
            recv_sem=recv2,
            device_id=(region_at(1 - o), b),
            device_id_type=MESH,
        )

    def copy3(d):
        return pltpu.make_async_remote_copy(
            src_ref=mstage.at[pl.ds(d * mig, mig)],
            dst_ref=mgot.at[pl.ds(me * mig, mig)],
            send_sem=send3,
            recv_sem=recv3,
            device_id=(r, d),
            device_id_type=MESH,
        )

    def await_all(ref, count, sem):
        whole = ref.at[pl.ds(0, count)]
        pltpu.make_async_copy(whole, whole, sem).wait()

    pl.semaphore_wait(barrier, len(peers))
    for o, d in peers:
        copy1(o, d).start()

    group = 8

    def build(step, carry):
        at = pl.ds(step * group, group)
        left[at], right[at], sums[at] = features(pts[at])
        return carry

    lax.fori_loop(0, blocks // group, build, 0)

    loads["pair_s"].wait()
    loads["touch_s"].wait()
    loads["lmask"].wait()
    loads["rmask"].wait()

    local_groups = pairs // LANES
    remote_groups = touch * recv_count // LANES
    count = local_groups + remote_groups
    early = local_groups // 2
    begin = early
    done = early + remote_groups

    def first_tile(i):
        shifted = jnp.where(
            i < begin, i, jnp.where(i < done, i + (local_groups - early), i - remote_groups)
        )
        return LANES * shifted

    tiles = pairs + touch * recv_count

    def members(first):
        remote = first >= pairs
        near = jnp.minimum(first, pairs - LANES)
        far = jnp.maximum(first - pairs, 0)
        t = far // recv_count
        q = far % recv_count
        found = []
        for u in range(LANES):
            found.append(
                (
                    jnp.where(remote, touch_s[t, q + u], pair_s[0, near + u]),
                    jnp.where(remote, blocks + q + u, pair_s[1, near + u]),
                    jnp.where(remote, pairs + touch * (q + u) + t, near + u),
                    first + u,
                )
            )
        return found

    def measure(first):
        for u, (a, b, _, _) in enumerate(members(first)):
            dists[u] = distance(left[b], right[a])

    def weigh(first):
        for u, (_, _, m, _) in enumerate(members(first)):
            s_hi, l_hi, s_lo, l_lo = split_weights(dists[u], masks[m])
            weights[u, 0, 0:width] = s_hi
            weights[u, 0, width:] = l_hi
            weights[u, 1, 0:width] = s_lo
            weights[u, 1, width:] = l_lo

    def put(at, value):
        terms[:, pl.ds(at, 1), :] = value[0:4].reshape(4, 1, width)

    def add(first):
        for u, (a, b, _, n) in enumerate(members(first)):
            on_a = on_b = None
            for piece in range(2):
                w = weights[u, piece]
                turned = jnp.concatenate([w[:width], w[width:]], axis=1)
                part_a = dot(sums[b], w, ALONG_J)
                part_b = dot(sums[a], turned, ALONG_I)
                on_a = part_a if on_a is None else on_a + part_a
                on_b = part_b if on_b is None else on_b + part_b
            put(n, combine(pts[a], on_a))
            term = combine(pts[b], on_b)
            put(tiles + n, term)
            bterm[n] = term

    def body(i, carry):
        for o in range(3):

            @pl.when(i == begin + o * (per // LANES))
            def _():
                count = sum(slots for peer in peers if peer[0] == o)
                await_all(got, count, recv1.at[o])
                for step in range(o * per // group, (o + 1) * per // group):
                    block = got[step * group : (step + 1) * group]
                    to = pl.ds(blocks + step * group, group)
                    pts[to] = block
                    left[to], _, sums[to] = features(block)

        last = i - 3 - (done - recv_count // LANES)

        @pl.when((last >= 0) & (last < recv_count // LANES))
        def _():
            for u in range(LANES):
                q = jnp.clip(last, 0, recv_count // LANES - 1) * LANES + u
                back[q] = sum(bterm[pairs + q + t * recv_count] for t in range(touch))

                @pl.when((q // per != 1) | (q % per // slots != me))
                def _():
                    copy2(q).start()

        add(first_tile(jnp.maximum(i - 2, 0)))
        weigh(first_tile(jnp.clip(i - 1, 0, count - 1)))
        measure(first_tile(jnp.minimum(i, count - 1)))
        return carry

    lax.fori_loop(0, count + 2, body, 0)
    for s in range(slots):
        ret[per + me * slots + s] = back[per + me * slots + s]

    loads["send_v"].wait()
    loads["touch_v"].wait()
    loads["pair_v"].wait()
    used = 2 * tiles + recv_count
    rows = terms.shape[1]

    def none(n):
        return jnp.full((1, n), -1, jnp.int32)

    index = jnp.concatenate(
        [pair_v[0:1]]
        + [touch_v[t : t + 1] for t in range(touch)]
        + [pair_v[1:2], none(touch * recv_count)]
        + [send_v[o, s : s + 1] for o in range(3) for s in range(slots)]
        + [none(rows - used)],
        axis=1,
    )
    here = lax.broadcasted_iota(jnp.int32, (blocks, rows), 0)
    pick = jnp.where(here == index, 1.0, 0.0).astype(BF16)
    await_all(ret, len(peers) * slots, recv2)

    for o in range(3):
        for s in range(slots):
            for d in range(nbulk):
                put(2 * tiles + (o * slots + s) * nbulk + d, ret[o * per + d * slots + s])
    terms[:, used:, :] = jnp.zeros((4, rows - used, width), F32)
    totals = []
    for k in range(4):
        parts = split3(terms[k])
        totals.append(
            sum(jnp.dot(pick, part.astype(BF16), preferred_element_type=F32) for part in parts)
        )
    loads["vel"].wait()
    loads["sto"].wait()
    for k in range(3):
        speed = vel_ref[k] + time_step * totals[k]
        nv_ref[k] = speed
        nf_ref[:, k, :] = fld_ref[:, k, :] + time_step * speed
    nf_ref[:, 3, :] = fld_ref[:, 3, :] + time_step * totals[3] / sto_ref[...]

    outs = [
        pltpu.make_async_copy(src, dst, out_sem.at[n])
        for n, (src, dst) in enumerate(
            ((nf_ref, nf_hbm), (nv_ref, nv_hbm), (arr_ref, arr_hbm))
        )
    ]
    outs[0].start()
    outs[1].start()
    loads["move_s"].wait()
    for d in range(nbulk):
        for m in range(mig):
            entry = move_s[m, 0, d]
            at = jnp.maximum(entry, 0)
            live = entry >= 0
            slot = d * mig + m
            mstage[slot, 0:4] = jnp.where(live, nf_ref[at], 0.0)
            for k in range(3):
                mstage[slot, 4 + k : 5 + k] = jnp.where(live, nv_ref[k, pl.ds(at, 1), :], 0.0)
                mstage[slot, 7 + k : 8 + k] = jnp.where(live, pos_ref[k, pl.ds(at, 1), :], 0.0)
            mstage[slot, 10:11] = jnp.where(live, sto_ref[pl.ds(at, 1), :], 0.0)
            mstage[slot, 11:16] = jnp.zeros((5, width), F32)
    others = [lax.rem(me + step, nbulk) for step in range(1, nbulk)]
    for d in others:
        copy3(d).start()
    for m in range(mig):
        mgot[me * mig + m] = mstage[me * mig + m]
    await_all(stage, len(peers) * slots, send1)
    await_all(back, len(peers) * slots, send2)
    await_all(mgot, len(others) * mig, recv3)
    for k in range(11):
        arr_ref[k] = mgot[:, k, :]
    outs[2].start()
    await_all(mstage, len(others) * mig, send3)
    for out in outs:
        out.wait()


def hand_out(*refs):
    sems = refs[9]
    into = [pltpu.make_async_copy(refs[n], refs[6 + n], sems.at[n]) for n in range(3)]
    out = [pltpu.make_async_copy(refs[6 + n], refs[3 + n], sems.at[3 + n]) for n in range(3)]
    for copy in into:
        copy.start()
    for n in range(3):
        into[n].wait()
        out[n].start()
    for copy in out:
        copy.wait()


def solution(mesh):
    nreg, nbulk = mesh.shape["region"], mesh.shape["bulk"]

    def per_device(
        positions,
        fields,
        storage,
        velocity,
        send_list,
        remote_local,
        remote_mask,
        local_pairs,
        local_mask,
        migrate_list,
    ):
        blocks, _, width = positions.shape
        slots = send_list.shape[3]
        recv_count, touch = remote_local.shape[1:]
        pairs = local_pairs.shape[1]
        mig = migrate_list.shape[2]
        per = nbulk * slots
        tiles = pairs + touch * recv_count
        held = blocks + recv_count
        rows = -(-(2 * tiles + recv_count) // 128) * 128
        sends = send_list[0].transpose(0, 2, 1)
        touches = remote_local[0].T
        pair_rows = local_pairs[0].T
        moves = migrate_list[0].T[:, None, :]
        hbm = pl.BlockSpec(memory_space=pltpu.HBM)
        out_shape = (
            jax.ShapeDtypeStruct((blocks, 4, width), F32),
            jax.ShapeDtypeStruct((3, blocks, width), F32),
            jax.ShapeDtypeStruct((11, nbulk * mig, width), F32),
        )
        dma = pltpu.SemaphoreType.DMA
        results = pl.pallas_call(
            functools.partial(kernel, nreg, nbulk),
            out_shape=out_shape,
            in_specs=[hbm] * 10,
            out_specs=(hbm, hbm, hbm),
            scratch_shapes=[
                pltpu.VMEM((blocks, 4, width), F32),
                pltpu.VMEM((3, blocks, width), F32),
                pltpu.VMEM((11, nbulk * mig, width), F32),
                pltpu.VMEM((3, blocks, width), F32),
                pltpu.VMEM((blocks, 4, width), F32),
                pltpu.VMEM((blocks, width), F32),
                pltpu.VMEM((3, blocks, width), F32),
                pltpu.SMEM(sends.shape, jnp.int32),
                pltpu.SMEM(touches.shape, jnp.int32),
                pltpu.SMEM(pair_rows.shape, jnp.int32),
                pltpu.SMEM(moves.shape, jnp.int32),
                pltpu.VMEM(sends.shape, jnp.int32),
                pltpu.VMEM(touches.shape, jnp.int32),
                pltpu.VMEM(pair_rows.shape, jnp.int32),
                pltpu.VMEM((tiles,) + local_mask.shape[2:], jnp.int32),
                pltpu.VMEM((held, 8, width), F32),
                pltpu.VMEM((recv_count, 8, width), F32),
                pltpu.VMEM((recv_count, 8, width), F32),
                pltpu.VMEM((recv_count, 8, width), F32),
                pltpu.VMEM((recv_count, 8, width), F32),
                pltpu.VMEM((nbulk * mig, 16, width), F32),
                pltpu.VMEM((nbulk * mig, 16, width), F32),
                pltpu.VMEM((held, width, 32), BF16),
                pltpu.VMEM((blocks, 32, width), BF16),
                pltpu.VMEM((held, 16, 2 * width), BF16),
                pltpu.VMEM((4, rows, width), F32),
                pltpu.VMEM((tiles, 8, width), F32),
                pltpu.VMEM((LANES, width, width), F32),
                pltpu.VMEM((LANES, 2, 2 * width, width), BF16),
                dma((13,)),
                dma((3,)),
                dma,
                dma((3,)),
                dma,
                dma,
                dma,
                dma,
            ],
            compiler_params=pltpu.CompilerParams(
                collective_id=0, has_side_effects=True, vmem_limit_bytes=64 << 20
            ),
        )(
            positions.transpose(1, 0, 2),
            fields,
            storage,
            velocity.transpose(1, 0, 2),
            sends,
            touches,
            pair_rows,
            moves,
            remote_mask[0].reshape((touch * recv_count,) + remote_mask.shape[3:]),
            local_mask[0],
        )
        new_fields, speed, arrived = pl.pallas_call(
            hand_out,
            out_shape=out_shape,
            in_specs=[hbm] * 3,
            out_specs=(hbm, hbm, hbm),
            scratch_shapes=[pltpu.VMEM(o.shape, F32) for o in out_shape] + [dma((6,))],
            compiler_params=pltpu.CompilerParams(vmem_limit_bytes=64 << 20),
        )(*results)
        return new_fields, speed.transpose(1, 0, 2), arrived.transpose(1, 0, 2)

    both = ("region", "bulk")
    return jax.shard_map(
        per_device,
        mesh=mesh,
        in_specs=(
            P(both, None, None),
            P(both, None, None),
            P(both, None),
            P(both, None, None),
            P(both, None, None, None),
            P(both, None, None),
            P(both, None, None, None, None),
            P(both, None, None),
            P(both, None, None, None),
            P(both, None, None),
        ),
        out_specs=(
            P(both, None, None),
            P(both, None, None),
            P(both, None, None),
        ),
        check_vma=False,
    )
```

```python
import functools

import jax
import jax.numpy as jnp
from jax import lax
from jax.experimental import pallas as pl
from jax.experimental.pallas import tpu as pltpu
from jax.sharding import PartitionSpec as P

MESH = pl.DeviceIdType.MESH
bond_stiff = 0.1
leak_gain = 0.5
time_step = 0.5
half_press = 0.025
LANES = 8
PACK = 4
F32 = jnp.float32
BF16 = jnp.bfloat16


def rows_of(shape):
    return lax.broadcasted_iota(jnp.int32, shape, len(shape) - 2)


def roll(x, by):
    return pltpu.roll(x, by % 8, x.ndim - 2)


def top(x):
    return x.astype(BF16).astype(F32)


def split3(x):
    first = top(x)
    rest = x - first
    second = top(rest)
    return first, second, rest - second


def features(block):
    row = rows_of(block.shape)
    half = jnp.where(row < 3, 0.5 * block, 0.0)
    norm = jnp.sum(half * half, axis=-2, keepdims=True) + 0.5
    h1, h2, h3 = split3(half)
    n1, n2, n3 = split3(norm)

    def eight(first, second, second_last, last):
        return jnp.where(
            row < 6, first + roll(second, 3), jnp.where(row == 6, second_last, last)
        )

    blank = jnp.zeros_like(half)
    b_rows = [eight(h1, h1, n1, 1.0), eight(h2, h2, n2, 1.0), eight(h1, h3, n3, 1.0), blank]
    a_rows = [
        eight(-2.0 * h1, -2.0 * h2, 1.0, n1),
        eight(-2.0 * h1, -2.0 * h2, 1.0, n2),
        eight(-2.0 * h3, -2.0 * h1, 1.0, n3),
        blank,
    ]
    flat = jnp.concatenate(b_rows, axis=-2).reshape(-1, PACK * 32, block.shape[-1])
    turned = [flat[n].T.astype(BF16) for n in range(flat.shape[0])]
    left = jnp.stack([t[:, 32 * m : 32 * m + 32] for t in turned for m in range(PACK)])
    right = jnp.concatenate(a_rows, axis=-2).astype(BF16)
    press = block[..., 6:7, :]
    moved = roll(block, -3)
    product = -0.25 * press * block
    product_top = top(product)
    moved_top = top(moved)
    block_top = top(block)
    press_top = top(press)
    spring_0 = jnp.where(row < 3, moved_top, jnp.where(row == 3, 1.0, 0.0))
    spring_1 = jnp.where((row >= 1) & (row < 4), roll(moved - moved_top, 1), 0.0)
    leak_0 = jnp.where(
        row < 3,
        product_top,
        jnp.where(
            row == 3, 0.0, jnp.where(row == 4, 1.0, jnp.where(row == 5, press_top, roll(block_top, 6)))
        ),
    )
    leak_1 = jnp.where(
        row == 0,
        roll(block_top, 6),
        jnp.where(
            row < 4,
            roll(product - product_top, 1),
            jnp.where(row == 4, press - press_top, roll(block - block_top, 5)),
        ),
    )
    sums = jnp.concatenate(
        [
            jnp.concatenate([spring_0, spring_1], axis=-2),
            jnp.concatenate([leak_0, leak_1], axis=-2),
        ],
        axis=-1,
    ).astype(BF16)
    return left, right, sums


def combine(block, out):
    row = rows_of(block.shape)
    r0, r1 = out[:8], out[8:]
    o1 = r0 + roll(r1, -1)
    o2 = r0[3:4]
    o4 = r0[4:5]
    o5 = r0[5:6] + r1[4:5]
    o3 = jnp.where(row < 2, roll(r0, 2), roll(r1, 2)) + roll(r1, 3)
    press = block[6:7]
    force = bond_stiff * (o1 - roll(block, -3) * o2) + half_press * (
        block * (press * o4 + o5) - press * o3
    )
    leak = leak_gain * (o5 - press * o4)
    return jnp.where(row < 3, force, jnp.where(row == 3, leak, 0.0))


ALONG_J = (((1,), (0,)), ((), ()))
ALONG_I = (((1,), (1,)), ((), ()))
dot = functools.partial(lax.dot_general, preferred_element_type=F32)


def distance(left_b, right_a):
    return dot(left_b, right_a, ALONG_J)


def split_weights(dist, packed):
    guess = pl.reciprocal(dist, approx=True)
    weight = guess * (2.0 - dist * guess)
    words, width = packed.shape
    bit = lax.shift_left(1, rows_of((1, 8, width)))
    intact = (jnp.broadcast_to(packed[:, None, :], (words, 8, width)) & bit) != 0
    intact = intact.reshape(words * 8, width)
    spring = jnp.where(intact, weight, 0.0)
    leak = jnp.where(intact, 0.0, weight)
    spring_hi = spring.astype(BF16)
    leak_hi = leak.astype(BF16)
    spring_lo = (spring - spring_hi.astype(F32)).astype(BF16)
    leak_lo = (leak - leak_hi.astype(F32)).astype(BF16)
    return spring_hi, leak_hi, spring_lo, leak_lo


def kernel(
    nreg,
    nbulk,
    pos_hbm,
    fld_hbm,
    sto_hbm,
    vel_hbm,
    send_hbm,
    touch_hbm,
    pair_hbm,
    move_hbm,
    rmask_hbm,
    lmask_hbm,
    nf_hbm,
    nv_hbm,
    arr_hbm,
    nf_ref,
    nv_ref,
    arr_ref,
    pos_ref,
    fld_ref,
    sto_ref,
    vel_ref,
    send_s,
    touch_s,
    pair_s,
    move_s,
    send_v,
    touch_v,
    pair_v,
    masks,
    pts,
    stage,
    got,
    back,
    ret,
    mstage,
    mgot,
    left,
    right,
    sums,
    terms,
    bterm,
    dists,
    weights,
    load_sem,
    out_sem,
    send1,
    recv1,
    send2,
    recv2,
    send3,
    recv3,
):
    blocks, width = sto_ref.shape
    slots = send_s.shape[1]
    per = nbulk * slots
    recv_count = 3 * per
    pairs = pair_s.shape[1]
    touch = touch_s.shape[0]
    mig = move_s.shape[0]
    r = lax.axis_index("region")
    me = lax.axis_index("bulk")

    def region_at(by):
        return lax.rem(r + by + nreg, nreg)

    peers = []
    for o in (0, 2, 1):
        for step in range(nbulk):
            if o == 1 and step == 0:
                continue
            peers.append((o, lax.rem(me + step, nbulk)))

    barrier = pltpu.get_barrier_semaphore()
    for o, d in peers:
        pl.semaphore_signal(barrier, inc=1, device_id=(region_at(o - 1), d), device_id_type=MESH)

    loads = {}
    for n, (name, src, dst) in enumerate(
        (
            ("send_s", send_hbm, send_s),
            ("pos", pos_hbm, pos_ref),
            ("fld", fld_hbm, fld_ref),
            ("pair_s", pair_hbm, pair_s),
            ("lmask", lmask_hbm, masks.at[pl.ds(0, pairs)]),
            ("touch_s", touch_hbm, touch_s),
            ("rmask", rmask_hbm, masks.at[pl.ds(pairs, touch * recv_count)]),
            ("vel", vel_hbm, vel_ref),
            ("sto", sto_hbm, sto_ref),
            ("move_s", move_hbm, move_s),
            ("send_v", send_hbm, send_v),
            ("touch_v", touch_hbm, touch_v),
            ("pair_v", pair_hbm, pair_v),
        )
    ):
        loads[name] = pltpu.make_async_copy(src, dst, load_sem.at[n])
        loads[name].start()

    loads["pos"].wait()
    loads["fld"].wait()
    for k in range(3):
        pts[0:blocks, k, :] = pos_ref[k]
    for k in range(4):
        pts[0:blocks, 3 + k, :] = fld_ref[:, k, :]
    pts[0:blocks, 7, :] = jnp.zeros((blocks, width), F32)
    loads["send_s"].wait()
    for o in range(3):
        for s in range(slots):
            for d in range(nbulk):
                stage[o * per + d * slots + s] = pts[send_s[o, s, d]]
    for s in range(slots):
        got[per + me * slots + s] = stage[per + me * slots + s]

    def span(ref, o, d):
        return ref.at[pl.ds(o * per + d * slots, slots)]

    def copy1(o, d):
        return pltpu.make_async_remote_copy(
            src_ref=span(stage, o, d),
            dst_ref=span(got, o, me),
            send_sem=send1,
            recv_sem=recv1,
            device_id=(region_at(o - 1), d),
            device_id_type=MESH,
        )

    def copy2(o, b):
        return pltpu.make_async_remote_copy(
            src_ref=span(back, o, b),
            dst_ref=span(ret, o, me),
            send_sem=send2,
            recv_sem=recv2,
            device_id=(region_at(1 - o), b),
            device_id_type=MESH,
        )

    def copy3(d):
        return pltpu.make_async_remote_copy(
            src_ref=mstage.at[pl.ds(d * mig, mig)],
            dst_ref=mgot.at[pl.ds(me * mig, mig)],
            send_sem=send3,
            recv_sem=recv3,
            device_id=(r, d),
            device_id_type=MESH,
        )

    def await_all(ref, count, sem):
        whole = ref.at[pl.ds(0, count)]
        pltpu.make_async_copy(whole, whole, sem).wait()

    pl.semaphore_wait(barrier, len(peers))
    for o, d in peers:
        copy1(o, d).start()

    group = 8

    def build(step, carry):
        at = pl.ds(step * group, group)
        left[at], right[at], sums[at] = features(pts[at])
        return carry

    lax.fori_loop(0, blocks // group, build, 0)

    loads["pair_s"].wait()
    loads["touch_s"].wait()
    loads["lmask"].wait()
    loads["rmask"].wait()

    local_groups = pairs // LANES
    remote_groups = touch * recv_count // LANES
    count = local_groups + remote_groups
    early = local_groups // 2
    begin = early
    done = early + remote_groups

    def first_tile(i):
        shifted = jnp.where(
            i < begin, i, jnp.where(i < done, i + (local_groups - early), i - remote_groups)
        )
        return LANES * shifted

    tiles = pairs + touch * recv_count

    def members(first):
        remote = first >= pairs
        near = jnp.minimum(first, pairs - LANES)
        far = jnp.maximum(first - pairs, 0)
        t = far // recv_count
        q = far % recv_count
        found = []
        for u in range(LANES):
            found.append(
                (
                    jnp.where(remote, touch_s[t, q + u], pair_s[0, near + u]),
                    jnp.where(remote, blocks + q + u, pair_s[1, near + u]),
                    jnp.where(remote, pairs + touch * (q + u) + t, near + u),
                    first + u,
                )
            )
        return found

    def measure(first):
        for u, (a, b, _, _) in enumerate(members(first)):
            dists[u] = distance(left[b], right[a])

    def weigh(first):
        for u, (_, _, m, _) in enumerate(members(first)):
            s_hi, l_hi, s_lo, l_lo = split_weights(dists[u], masks[m])
            weights[u, 0, 0:width] = s_hi
            weights[u, 0, width:] = l_hi
            weights[u, 1, 0:width] = s_lo
            weights[u, 1, width:] = l_lo

    def put(at, value):
        terms[:, pl.ds(at, 1), :] = value[0:4].reshape(4, 1, width)

    def add(first):
        for u, (a, b, _, n) in enumerate(members(first)):
            on_a = on_b = None
            for piece in range(2):
                w = weights[u, piece]
                turned = jnp.concatenate([w[:width], w[width:]], axis=1)
                part_a = dot(sums[b], w, ALONG_J)
                part_b = dot(sums[a], turned, ALONG_I)
                on_a = part_a if on_a is None else on_a + part_a
                on_b = part_b if on_b is None else on_b + part_b
            put(n, combine(pts[a], on_a))
            term = combine(pts[b], on_b)
            put(tiles + n, term)
            bterm[n] = term

    def body(i, carry):
        @pl.when(i == begin)
        def _():
            await_all(got, len(peers) * slots, recv1)
            for step in range(recv_count // group):
                block = got[step * group : (step + 1) * group]
                to = pl.ds(blocks + step * group, group)
                pts[to] = block
                left[to], _, sums[to] = features(block)

        @pl.when(i == done + 2)
        def _():
            for o in range(3):
                for s in range(per):
                    at = pairs + o * per + s
                    back[o * per + s] = sum(bterm[at + t * recv_count] for t in range(touch))
            for o, d in peers:
                copy2(o, d).start()

        add(first_tile(jnp.maximum(i - 2, 0)))
        weigh(first_tile(jnp.clip(i - 1, 0, count - 1)))
        measure(first_tile(jnp.minimum(i, count - 1)))
        return carry

    lax.fori_loop(0, count + 2, body, 0)
    for s in range(slots):
        ret[per + me * slots + s] = back[per + me * slots + s]

    loads["send_v"].wait()
    loads["touch_v"].wait()
    loads["pair_v"].wait()
    used = 2 * tiles + recv_count
    rows = terms.shape[1]

    def none(n):
        return jnp.full((1, n), -1, jnp.int32)

    index = jnp.concatenate(
        [pair_v[0:1]]
        + [touch_v[t : t + 1] for t in range(touch)]
        + [pair_v[1:2], none(touch * recv_count)]
        + [send_v[o, s : s + 1] for o in range(3) for s in range(slots)]
        + [none(rows - used)],
        axis=1,
    )
    here = lax.broadcasted_iota(jnp.int32, (blocks, rows), 0)
    pick = jnp.where(here == index, 1.0, 0.0).astype(BF16)
    await_all(ret, len(peers) * slots, recv2)

    for o in range(3):
        for s in range(slots):
            for d in range(nbulk):
                put(2 * tiles + (o * slots + s) * nbulk + d, ret[o * per + d * slots + s])
    terms[:, used:, :] = jnp.zeros((4, rows - used, width), F32)
    totals = []
    for k in range(4):
        parts = split3(terms[k])
        totals.append(
            sum(jnp.dot(pick, part.astype(BF16), preferred_element_type=F32) for part in parts)
        )
    loads["vel"].wait()
    loads["sto"].wait()
    for k in range(3):
        speed = vel_ref[k] + time_step * totals[k]
        nv_ref[k] = speed
        nf_ref[:, k, :] = fld_ref[:, k, :] + time_step * speed
    nf_ref[:, 3, :] = fld_ref[:, 3, :] + time_step * totals[3] / sto_ref[...]

    outs = [
        pltpu.make_async_copy(src, dst, out_sem.at[n])
        for n, (src, dst) in enumerate(
            ((nf_ref, nf_hbm), (nv_ref, nv_hbm), (arr_ref, arr_hbm))
        )
    ]
    outs[0].start()
    outs[1].start()
    loads["move_s"].wait()
    for d in range(nbulk):
        for m in range(mig):
            entry = move_s[m, 0, d]
            at = jnp.maximum(entry, 0)
            live = entry >= 0
            slot = d * mig + m
            mstage[slot, 0:4] = jnp.where(live, nf_ref[at], 0.0)
            for k in range(3):
                mstage[slot, 4 + k : 5 + k] = jnp.where(live, nv_ref[k, pl.ds(at, 1), :], 0.0)
                mstage[slot, 7 + k : 8 + k] = jnp.where(live, pos_ref[k, pl.ds(at, 1), :], 0.0)
            mstage[slot, 10:11] = jnp.where(live, sto_ref[pl.ds(at, 1), :], 0.0)
            mstage[slot, 11:16] = jnp.zeros((5, width), F32)
    others = [lax.rem(me + step, nbulk) for step in range(1, nbulk)]
    for d in others:
        copy3(d).start()
    for m in range(mig):
        mgot[me * mig + m] = mstage[me * mig + m]
    await_all(stage, len(peers) * slots, send1)
    await_all(back, len(peers) * slots, send2)
    await_all(mgot, len(others) * mig, recv3)
    for k in range(11):
        arr_ref[k] = mgot[:, k, :]
    outs[2].start()
    await_all(mstage, len(others) * mig, send3)
    for out in outs:
        out.wait()


def hand_out(*refs):
    sems = refs[9]
    into = [pltpu.make_async_copy(refs[n], refs[6 + n], sems.at[n]) for n in range(3)]
    out = [pltpu.make_async_copy(refs[6 + n], refs[3 + n], sems.at[3 + n]) for n in range(3)]
    for copy in into:
        copy.start()
    for n in range(3):
        into[n].wait()
        out[n].start()
    for copy in out:
        copy.wait()


def solution(mesh):
    nreg, nbulk = mesh.shape["region"], mesh.shape["bulk"]

    def per_device(
        positions,
        fields,
        storage,
        velocity,
        send_list,
        remote_local,
        remote_mask,
        local_pairs,
        local_mask,
        migrate_list,
    ):
        blocks, _, width = positions.shape
        slots = send_list.shape[3]
        recv_count, touch = remote_local.shape[1:]
        pairs = local_pairs.shape[1]
        mig = migrate_list.shape[2]
        per = nbulk * slots
        tiles = pairs + touch * recv_count
        held = blocks + recv_count
        rows = -(-(2 * tiles + recv_count) // 128) * 128
        sends = send_list[0].transpose(0, 2, 1)
        touches = remote_local[0].T
        pair_rows = local_pairs[0].T
        moves = migrate_list[0].T[:, None, :]
        hbm = pl.BlockSpec(memory_space=pltpu.HBM)
        out_shape = (
            jax.ShapeDtypeStruct((blocks, 4, width), F32),
            jax.ShapeDtypeStruct((3, blocks, width), F32),
            jax.ShapeDtypeStruct((11, nbulk * mig, width), F32),
        )
        dma = pltpu.SemaphoreType.DMA
        results = pl.pallas_call(
            functools.partial(kernel, nreg, nbulk),
            out_shape=out_shape,
            in_specs=[hbm] * 10,
            out_specs=(hbm, hbm, hbm),
            scratch_shapes=[
                pltpu.VMEM((blocks, 4, width), F32),
                pltpu.VMEM((3, blocks, width), F32),
                pltpu.VMEM((11, nbulk * mig, width), F32),
                pltpu.VMEM((3, blocks, width), F32),
                pltpu.VMEM((blocks, 4, width), F32),
                pltpu.VMEM((blocks, width), F32),
                pltpu.VMEM((3, blocks, width), F32),
                pltpu.SMEM(sends.shape, jnp.int32),
                pltpu.SMEM(touches.shape, jnp.int32),
                pltpu.SMEM(pair_rows.shape, jnp.int32),
                pltpu.SMEM(moves.shape, jnp.int32),
                pltpu.VMEM(sends.shape, jnp.int32),
                pltpu.VMEM(touches.shape, jnp.int32),
                pltpu.VMEM(pair_rows.shape, jnp.int32),
                pltpu.VMEM((tiles,) + local_mask.shape[2:], jnp.int32),
                pltpu.VMEM((held, 8, width), F32),
                pltpu.VMEM((recv_count, 8, width), F32),
                pltpu.VMEM((recv_count, 8, width), F32),
                pltpu.VMEM((recv_count, 8, width), F32),
                pltpu.VMEM((recv_count, 8, width), F32),
                pltpu.VMEM((nbulk * mig, 16, width), F32),
                pltpu.VMEM((nbulk * mig, 16, width), F32),
                pltpu.VMEM((held, width, 32), BF16),
                pltpu.VMEM((blocks, 32, width), BF16),
                pltpu.VMEM((held, 16, 2 * width), BF16),
                pltpu.VMEM((4, rows, width), F32),
                pltpu.VMEM((tiles, 8, width), F32),
                pltpu.VMEM((LANES, width, width), F32),
                pltpu.VMEM((LANES, 2, 2 * width, width), BF16),
                dma((13,)),
                dma((3,)),
                dma,
                dma,
                dma,
                dma,
                dma,
                dma,
            ],
            compiler_params=pltpu.CompilerParams(
                collective_id=0, has_side_effects=True, vmem_limit_bytes=64 << 20
            ),
        )(
            positions.transpose(1, 0, 2),
            fields,
            storage,
            velocity.transpose(1, 0, 2),
            sends,
            touches,
            pair_rows,
            moves,
            remote_mask[0].reshape((touch * recv_count,) + remote_mask.shape[3:]),
            local_mask[0],
        )
        new_fields, speed, arrived = pl.pallas_call(
            hand_out,
            out_shape=out_shape,
            in_specs=[hbm] * 3,
            out_specs=(hbm, hbm, hbm),
            scratch_shapes=[pltpu.VMEM(o.shape, F32) for o in out_shape] + [dma((6,))],
            compiler_params=pltpu.CompilerParams(vmem_limit_bytes=64 << 20),
        )(*results)
        return new_fields, speed.transpose(1, 0, 2), arrived.transpose(1, 0, 2)

    both = ("region", "bulk")
    return jax.shard_map(
        per_device,
        mesh=mesh,
        in_specs=(
            P(both, None, None),
            P(both, None, None),
            P(both, None),
            P(both, None, None),
            P(both, None, None, None),
            P(both, None, None),
            P(both, None, None, None, None),
            P(both, None, None),
            P(both, None, None, None),
            P(both, None, None),
        ),
        out_specs=(
            P(both, None, None),
            P(both, None, None),
            P(both, None, None),
        ),
        check_vma=False,
    )
```
